32 devices in a mesh: ctx: 8 (over z, y), head: 4 (over x, core).
Axes of the slice: x: 2, y: 2, z: 4, core: 2. Of those that a mesh axis runs over, the one named last changes fastest.
Arguments:
- queries: bfloat16 [12288, 2048], P('ctx', 'head'), may hold values from -20 to 20
- keys: bfloat16 [12288, 2048], P('ctx', 'head'), may hold values from -20 to 20
- values: bfloat16 [12288, 2048], P('ctx', 'head'), may hold values from -6 to 6
- offsets: int32 [3, 16], replicated, may hold values from 0 to 7, as said below
- out_weight: bfloat16 [2048, 2048], replicated, may hold values from -1.1953125 to 1.1953125
Outputs:
- mixed: bfloat16 [12288, 2048], P(('ctx', 'head'))
The draws below stay inside these ranges and needn't reach their ends.
Inputs may be any that keep to these rules, and one draw needn't show every extreme that they name: `offsets`: each offset of row k - 1 lies in 0 to 2^k - 1; in the last row every value of that range occurs.
All inputs are finite; a program needn't handle non-finite values.
Results may differ from the reference program's by a relative error of at most 0.0053.
Values may be sent and summed in bfloat16 or wider, within the bound.
No kernel may reach another device: no remote copies, remote signals or barrier semaphores. Data moves between devices by JAX's collectives and lax.ppermute only.
A program may use at most 192 MiB of HBM per device.

```python
import math
import jax
import jax.numpy as jnp
from jax import lax

D = 2048
HEADS = 16
DH = 128
TOK_DEV = 1536
LEVELS = 4
L = 12288


def drawn(key, salt):
    return jnp.clip(jax.random.normal(jax.random.fold_in(key, salt), (L, D), jnp.float32), -4.0, 4.0)


def draw_queries(key, part):
    entries = drawn(key, 21)
    return entries.astype(jnp.bfloat16)


def draw_keys(key, part):
    entries = drawn(key, 23)
    return entries.astype(jnp.bfloat16)


def draw_offsets(key, part):
    listed = []
    for level_index in range(1, LEVELS):
        order = jax.random.permutation(jax.random.fold_in(key, 30 + level_index), HEADS)
        listed.append(order % 2 ** level_index)
    return jnp.stack(listed).astype(jnp.int32)


def block_levels(rng, extent, shards, low, high):
    def one(dim, blocks):
        draws = jax.random.uniform(jax.random.fold_in(jax.random.fold_in(rng, 6), dim), (blocks,), jnp.float32, low / len(shards), high / len(shards))
        return jnp.repeat(jnp.exp(draws), extent[dim] // blocks).reshape((-1,) + (1,) * (len(extent) - dim - 1))

    factor_of = one(*shards[0])
    for cut in shards[1:]:
        factor_of = factor_of * one(*cut)
    return factor_of


def bell_draw(own_key, dims, width, most, shards=(), held_as=jnp.bfloat16):
    factor_of = block_levels(own_key, dims, shards, -0.22, 0.18) if shards else 1.0
    drawn = jax.random.normal(own_key, dims, jnp.float32) * width * factor_of
    return jnp.minimum(jnp.maximum(drawn, -most), most).astype(held_as)


def setup_inputs(seed: int = 0) -> dict:
    seeds = jax.random.split(jax.random.key(seed), 6)
    return {
        "queries": draw_queries(jax.random.fold_in(seeds[5], 71), 0),
        "keys": draw_keys(jax.random.fold_in(seeds[5], 71), 0),
        "values": bell_draw(seeds[2], (L, D), 1.0, 6.0, ((0, 8), (1, 4))),
        "offsets": draw_offsets(jax.random.fold_in(seeds[5], 71), 0),
        "out_weight": bell_draw(seeds[4], (D, D), 0.2, 1.1953125),
    }


NEG_FILL = -1e+30

def attend_one(query_rows, key_rows, value_rows):
    number = query_rows.shape[0]
    scores = jnp.dot(query_rows, key_rows.T, preferred_element_type=jnp.float32) * (1.0 / math.sqrt(DH))
    index_rows = jnp.arange(number)
    scores = jnp.where(index_rows[:, None] >= index_rows[None, :], scores, NEG_FILL)
    row_max = lax.optimization_barrier(jnp.max(scores, axis=1))
    weights = jnp.exp(scores - row_max[:, None])
    row_sum = lax.optimization_barrier(jnp.sum(weights, axis=1))
    weighted = jnp.dot(weights.astype(jnp.bfloat16), value_rows, preferred_element_type=jnp.float32)
    return (row_max, row_sum, weighted)

def level_terms(query_heads, key_heads, value_heads, shifts, dilation):
    segments = query_heads.shape[0] // (TOK_DEV * dilation)
    hits = jnp.arange(dilation)[:, None] == shifts[None, :]

    def select(source):
        shaped = source.reshape(segments, TOK_DEV, dilation, HEADS, DH)
        return lax.optimization_barrier(jnp.sum(jnp.where(hits[None, None, :, :, None], shaped, jnp.zeros((), source.dtype)), axis=2))
    picked_q, picked_k, picked_v = (select(query_heads), select(key_heads), select(value_heads))

    def per_segment(items):
        seg_q, seg_k, seg_v = items

        def per_head(head_index):
            return attend_one(seg_q[:, head_index], seg_k[:, head_index], seg_v[:, head_index])
        return lax.map(per_head, jnp.arange(HEADS))
    row_max, row_sum, weighted = lax.map(per_segment, (picked_q, picked_k, picked_v))
    row_max = jnp.transpose(row_max, (0, 2, 1))
    row_sum = jnp.transpose(row_sum, (0, 2, 1))
    weighted = jnp.transpose(weighted, (0, 2, 1, 3))
    full_max = jnp.where(hits[None, None], row_max[:, :, None, :], NEG_FILL).reshape(-1, HEADS)
    full_sum = jnp.where(hits[None, None], row_sum[:, :, None, :], 0.0).reshape(-1, HEADS)
    full_out = jnp.where(hits[None, None, :, :, None], weighted[:, :, None], 0.0).reshape(-1, HEADS, DH)
    return (full_max, full_sum, full_out)

def merge_levels(running, fresh):
    new_max = jnp.maximum(running[0], fresh[0])
    old_scale = jnp.exp(running[0] - new_max)
    new_scale = jnp.exp(fresh[0] - new_max)
    new_sum = running[1] * old_scale + fresh[1] * new_scale
    new_out = running[2] * old_scale[:, :, None] + fresh[2] * new_scale[:, :, None]
    return (new_max, new_sum, new_out)

def reference(queries, keys, values, offsets, out_weight):
    query_heads = queries.reshape(-1, HEADS, DH)
    key_heads = keys.reshape(-1, HEADS, DH)
    value_heads = values.reshape(-1, HEADS, DH)
    running = level_terms(query_heads, key_heads, value_heads, jnp.zeros((HEADS,), jnp.int32), 1)
    for level_index in range(1, LEVELS):
        fresh = level_terms(query_heads, key_heads, value_heads, offsets[level_index - 1], 2 ** level_index)
        running = merge_levels(running, fresh)
    attended = (running[2] / running[1][:, :, None]).astype(jnp.bfloat16).reshape(-1, HEADS * DH)
    return jnp.dot(attended, out_weight, preferred_element_type=jnp.float32).astype(jnp.bfloat16)
```

```python
import functools
import math

import jax
import jax.numpy as jnp
from jax import lax
from jax.experimental import pallas as pl
from jax.experimental.pallas import tpu as pltpu
from jax.sharding import PartitionSpec as P

DH = 128
RES = 8
SUB = 16
BLK = RES * SUB
NEG = -1e30
RATE = math.log2(math.e) / math.sqrt(DH)
BF16 = jnp.bfloat16
F32 = jnp.float32
VMEM_LIMIT = 48 * 1024 * 1024


def iota(shape, dim):
    return lax.broadcasted_iota(jnp.int32, shape, dim)


def regroup_matrix(inverse):
    row, col = iota((BLK, BLK), 0), iota((BLK, BLK), 1)
    if inverse:
        hit = col == (row % RES) * SUB + row // RES
    else:
        hit = col == (row % SUB) * RES + row // SUB
    return jnp.where(hit, 1.0, 0.0).astype(BF16)


def causal_bias(position, size):
    rows = position(iota((size, size), 0))
    cols = position(iota((size, size), 1))
    return jnp.where(cols <= rows, 0.0, NEG)


def attend(q, blocks):
    scores, top = [], None
    for k, _, bias in blocks:
        s = lax.dot_general(q, k, (((1,), (1,)), ((), ())), preferred_element_type=F32)
        if bias is not None:
            s = s + bias
        scores.append(s)
    if all(s.shape == scores[0].shape for s in scores):
        wide = scores[0]
        for s in scores[1:]:
            wide = jnp.maximum(wide, s)
        top = jnp.max(wide, axis=1, keepdims=True)
    else:
        for s in scores:
            m = jnp.max(s, axis=1, keepdims=True)
            top = m if top is None else jnp.maximum(top, m)
    total = None
    for s, (_, v, _) in zip(scores, blocks):
        p = jnp.exp2((s - top) * RATE).astype(BF16)
        with_ones = jnp.concatenate([v, jnp.ones(v.shape, BF16)], axis=1)
        part = jnp.dot(p, with_ones, preferred_element_type=F32)
        total = part if total is None else total + part
    row_sum = total[:, DH:]
    return total[:, :DH] / row_sum, top * RATE + jnp.log2(row_sum)


def merge(parts):
    top = parts[0][1]
    for _, lse in parts[1:]:
        top = jnp.maximum(top, lse)
    out, weight = 0.0, 0.0
    for o, lse in parts:
        w = jnp.exp2(lse - top)
        out += o * w
        weight += w
    return out / weight, top + jnp.log2(weight)


def rows_of(ref, level, shift, first=0, count=None):
    count = ref.shape[0] - first if count is None else count
    return [
        ref[pl.ds(first, count), shift + j * 2**level].reshape(count * SUB, DH)
        for j in range(RES // 2**level)
    ]


def prep_kernel(off_ref, q_ref, k_ref, v_ref, qt, kt, vt, *sends):
    groups = len(sends) // 4
    heads = qt.shape[0]
    blocks = qt.shape[1]
    first = lax.axis_index("head") * heads
    turn = regroup_matrix(False)
    for src, dst in ((q_ref, qt), (k_ref, kt), (v_ref, vt)):
        for b in range(blocks):
            x = jnp.dot(turn, src[b * BLK : (b + 1) * BLK, :], preferred_element_type=F32)
            x = x.astype(BF16)
            for h in range(heads):
                dst[h, b] = x[:, h * DH : (h + 1) * DH].reshape(RES, SUB, DH)
    per = heads // groups
    for g in range(groups):
        q1, q23, kv2, kv3 = sends[4 * g : 4 * g + 4]
        for n in range(per):
            h = g * per + n
            o1, o2, o3 = (off_ref[lv, first + h] for lv in range(3))
            for j, x in enumerate(rows_of(qt.at[h], 1, o1)):
                q1[n, j] = x
            for j, x in enumerate(rows_of(qt.at[h], 2, o2) + rows_of(qt.at[h], 3, o3)):
                q23[n, j] = x
            for i, src in enumerate((kt, vt)):
                for j, x in enumerate(rows_of(src.at[h], 2, o2)):
                    kv2[n, i, j] = x
                kv3[n, i] = rows_of(src.at[h], 3, o3)[0]


def own_kernel(first_head, off_ref, qt, kt, vt, out, lse):
    qt, kt, vt, out, lse = (r.at[0] for r in (qt, kt, vt, out, lse))
    blocks = qt.shape[0]
    head = lax.axis_index("head") * HEADS_HERE + first_head + pl.program_id(0)
    step = 2
    size = step * BLK
    bias = causal_bias(lambda r: r // BLK * BLK + r % SUB * RES + r % BLK // SUB, size)
    load = lambda ref, n: ref[n * step : (n + 1) * step].reshape(size, DH)
    for n in range(blocks // step):
        parts = [
            (load(kt, i), load(vt, i), bias if i == n else None) for i in range(n + 1)
        ]
        o, s = attend(load(qt, n), parts)
        out[n * step : (n + 1) * step] = o.reshape(step, RES, SUB, DH)
        lse[n * step : (n + 1) * step] = s.reshape(step, RES, SUB, DH)
    shift = off_ref[0, head]
    step = 4
    rows = step * SUB
    slices = RES // 2
    size = rows * slices
    bias = causal_bias(lambda r: r % rows * slices + r // rows, size)
    load = lambda ref, n: jnp.concatenate(rows_of(ref, 1, shift, n * step, step), axis=0)
    for n in range(blocks // step):
        parts = [
            (load(kt, i), load(vt, i), bias if i == n else None) for i in range(n + 1)
        ]
        o, s = attend(load(qt, n), parts)
        o, s = merge([(o, s), (load(out, n), load(lse, n))])
        for j in range(slices):
            at = (pl.ds(n * step, step), shift + 2 * j)
            out[at] = o[j * rows : (j + 1) * rows].reshape(step, SUB, DH)
            lse[at] = s[j * rows : (j + 1) * rows].reshape(step, SUB, DH)


def put_stat(slab, stat, place):
    lane = iota(stat.shape, 1)
    rest = stat
    now = slab[...]
    for i in range(3):
        piece = rest.astype(BF16)
        rest = rest - piece.astype(F32)
        now = jnp.where(lane == place + 32 * i, piece, now)
    slab[...] = now


def get_stat(slab, place):
    lane = iota(slab.shape, 1)
    hit = (lane == place) | (lane == place + 32) | (lane == place + 64)
    return jnp.sum(jnp.where(hit, slab[...].astype(F32), 0.0), axis=1, keepdims=True)


def lower_kernel(first_head, off_ref, q1, kt, vt, msg):
    here = pl.program_id(0)
    head = lax.axis_index("head") * HEADS_HERE + first_head + here

    @pl.when(here == 0)
    def _():
        msg[msg.shape[0] - 1] = jnp.zeros(msg.shape[1:], BF16)

    @pl.when(lax.axis_index("ctx") % 2 == 0)
    def _():
        shift = off_ref[0, head]
        count = RES // 2
        k = jnp.concatenate(rows_of(kt.at[0], 1, shift), axis=0)
        v = jnp.concatenate(rows_of(vt.at[0], 1, shift), axis=0)
        rows = q1.shape[2]
        for pair in range(count // 2):
            q = q1[0, 2 * pair : 2 * pair + 2].reshape(2 * rows, DH)
            o, s = attend(q, [(k, v, None)])
            for i in range(2):
                j = 2 * pair + i
                place = here * count + j
                msg[place] = o[i * rows : (i + 1) * rows].astype(BF16)
                put_stat(msg.at[msg.shape[0] - 1], s[i * rows : (i + 1) * rows], place)


def level_kernel(level, first_head, off_ref, qt, kt, vt, q23, before, out, lse, msg):
    here = pl.program_id(0)
    head = lax.axis_index("head") * HEADS_HERE + first_head + here
    ctx = lax.axis_index("ctx")
    shift = off_ref[level - 1, head]
    count = RES // 2**level
    rows = q23.shape[2]
    size = count * rows

    @pl.when(here == 0)
    def _():
        msg[msg.shape[0] - 1] = jnp.zeros(msg.shape[1:], BF16)

    def whole(ref):
        return jnp.concatenate(rows_of(ref.at[0], level, shift), axis=0)

    own_k, own_v = whole(kt), whole(vt)
    base = 0 if level == 2 else 2
    past = []
    if level == 2:
        allowed = ctx // 2 % 2 == 1
        past.append(
            (
                before[0, 0].reshape(size, DH),
                before[0, 1].reshape(size, DH),
                jnp.where(allowed, 0.0, NEG),
            )
        )
    else:
        for z in range(before.shape[0] - 1):
            past.append((before[z, 0, 0], before[z, 0, 1], jnp.where(z < ctx // 2 % 4, 0.0, NEG)))
    triangle = causal_bias(lambda r: r % rows * count + r // rows, size)
    o, s = attend(whole(qt), past + [(own_k, own_v, triangle)])
    for j in range(count):
        out[0, j] = o[j * rows : (j + 1) * rows]
        lse[0, j] = s[j * rows : (j + 1) * rows]
    later = jnp.where(ctx % 2 == 0, 0.0, NEG)
    q = q23[0, base : base + count].reshape(size, DH)
    o, s = attend(q, past + [(own_k, own_v, later)])
    for j in range(count):
        place = here * count + j
        msg[place] = o[j * rows : (j + 1) * rows].astype(BF16)
        put_stat(msg.at[msg.shape[0] - 1], s[j * rows : (j + 1) * rows], place)


def merge_kernel(
    first_head, off_ref, o0, s0, o2, s2, o3, s3, m1, m2, m3, dest0, dest1, dest2, dest3, acc, sums
):
    here = pl.program_id(0)
    head = lax.axis_index("head") * HEADS_HERE + first_head + here
    ctx = lax.axis_index("ctx")
    blocks, rows = o0.shape[1], o0.shape[1] * SUB
    shifts = [off_ref[lv, head] for lv in range(3)]
    acc[...] = o0[0]
    sums[...] = s0[0]
    for level, msg, own in ((1, m1, None), (2, m2, (o2, s2)), (3, m3, (o3, s3))):
        count = RES // 2**level
        slab = msg.at[msg.shape[0] - 1]
        for j in range(count):
            at = shifts[level - 1] + j * 2**level
            place = here * count + j
            stat = get_stat(slab, place)
            if level == 1:
                stat = jnp.where(ctx % 2 == 1, stat, NEG)
            parts = [
                (acc[:, at].reshape(rows, DH), sums[:, at].reshape(rows, DH)),
                (msg[place].astype(F32), jnp.broadcast_to(stat, (rows, DH))),
            ]
            if own is not None:
                parts.append((own[0][0, j], own[1][0, j]))
            o, s = merge(parts)
            acc[:, at] = o.reshape(blocks, SUB, DH)
            sums[:, at] = s.reshape(blocks, SUB, DH)
    mine = lax.axis_index("head")
    per = blocks // 4
    for t, dest in enumerate((dest0, dest1, dest2, dest3)):
        at = (mine ^ t) * per
        dest[...] = acc[pl.ds(at, per)].reshape(per * BLK, DH).astype(BF16)


def project_kernel(a0, a1, a2, a3, w_ref, out, plain):
    size = a0.shape[1]

    @pl.when(pl.program_id(0) == 0)
    def _():
        back = regroup_matrix(True)
        for t, src in enumerate((a0, a1, a2, a3)):
            for b in range(src.shape[0] // BLK):
                at = slice(b * BLK, (b + 1) * BLK)
                x = jnp.dot(back, src[at, :], preferred_element_type=F32)
                plain[at, t * size : (t + 1) * size] = x.astype(BF16)

    mine = lax.axis_index("head")
    total = None
    for t in range(4):
        w = w_ref[pl.ds(pl.multiple_of((mine ^ t) * size, size), size), :]
        part = jnp.dot(
            plain[:, t * size : (t + 1) * size], w, preferred_element_type=F32
        )
        total = part if total is None else total + part
    out[...] = total.astype(BF16)


HEADS_HERE = 4
SMEM = pl.BlockSpec(memory_space=pltpu.SMEM)


def shape(*dims, dtype=BF16):
    return jax.ShapeDtypeStruct(dims, dtype)


def per_head(array):
    rest = array.shape[1:]
    return pl.BlockSpec((1, *rest), lambda h, n=len(rest): (h,) + (0,) * n)


def from_head(array, first):
    rest = array.shape[1:]
    return pl.BlockSpec((1, *rest), lambda h, n=len(rest): (h + first,) + (0,) * n)


def whole(array):
    return pl.BlockSpec(array.shape, lambda h, n=len(array.shape): (0,) * n)


def params():
    return pltpu.CompilerParams(vmem_limit_bytes=VMEM_LIMIT)


def cost(macs, moved):
    return pl.CostEstimate(flops=2 * macs, bytes_accessed=moved, transcendentals=0)


GROUPS = 1


def body(queries, keys, values, offsets, out_weight):
    rows_here, width = queries.shape
    blocks = rows_here // BLK
    heads = width // DH
    per = heads // GROUPS
    slots = rows_here // RES
    regrouped = shape(heads, blocks, RES, SUB, DH)
    sends = []
    for _ in range(GROUPS):
        sends += [
            shape(per, 4, slots, DH),
            shape(per, 3, slots, DH),
            shape(per, 2, 2, slots, DH),
            shape(per, 2, slots, DH),
        ]
    vmem = pl.BlockSpec(memory_space=pltpu.VMEM)
    qt, kt, vt, *sends = pl.pallas_call(
        prep_kernel,
        in_specs=[SMEM, vmem, vmem, vmem],
        out_specs=[vmem] * (3 + 4 * GROUPS),
        out_shape=[regrouped] * 3 + sends,
        compiler_params=params(),
        cost_estimate=cost(3 * rows_here * BLK * width, 12 * 2**20),
        name="prep",
    )(offsets, queries, keys, values)

    ctx_size = lax.axis_size("ctx")
    swap = [(i, i ^ 1) for i in range(ctx_size)]
    down = [(i + 1, i) for i in range(0, ctx_size, 2)]
    up = [(i, i + 1) for i in range(0, ctx_size, 2)]
    column2 = [(i, i + 2) for i in range(ctx_size) if i // 2 % 2 == 0]
    column4 = [
        [s + y + 2 * z for z in range(4)] for s in range(0, ctx_size, 8) for y in range(2)
    ]
    pieces = []
    for g in range(GROUPS):
        q1, q23, kv2, kv3 = sends[4 * g : 4 * g + 4]
        first = g * per
        q1 = lax.ppermute(q1, "ctx", down)
        q23 = lax.ppermute(q23, "ctx", swap)
        kv2 = lax.ppermute(kv2, "ctx", column2)
        kv3 = lax.all_gather(kv3, "ctx", axis_index_groups=column4)
        o0, s0 = pl.pallas_call(
            functools.partial(own_kernel, first),
            grid=(per,),
            in_specs=[SMEM] + [from_head(x, first) for x in (qt, kt, vt)],
            out_specs=[per_head(shape(per, blocks, RES, SUB, DH))] * 2,
            out_shape=[shape(per, blocks, RES, SUB, DH, dtype=F32)] * 2,
            compiler_params=params(),
            cost_estimate=cost(per * 6 * 2**28, 10 * 2**20),
            name="own",
        )(offsets, qt, kt, vt)
        msg1 = shape(per * 4 + 1, slots, DH)
        m1 = pl.pallas_call(
            functools.partial(lower_kernel, first),
            grid=(per,),
            in_specs=[SMEM, per_head(q1)] + [from_head(x, first) for x in (kt, vt)],
            out_specs=whole(msg1),
            out_shape=msg1,
            compiler_params=params(),
            cost_estimate=cost(per * 3 * 2**28, 4 * 2**20),
            name="lower",
        )(offsets, q1, kt, vt)
        m1 = lax.ppermute(m1, "ctx", up)
        levels = []
        for level, before in ((2, kv2), (3, kv3)):
            count = RES // 2**level
            own = shape(per, count, slots, DH, dtype=F32)
            msg = shape(per * count + 1, slots, DH)
            if level == 2:
                spec = per_head(before)
            else:
                spec = pl.BlockSpec(
                    (before.shape[0], 1, *before.shape[2:]), lambda h: (0, h, 0, 0, 0)
                )
            o, s, m = pl.pallas_call(
                functools.partial(level_kernel, level, first),
                grid=(per,),
                in_specs=[SMEM]
                + [from_head(x, first) for x in (qt, kt, vt)]
                + [per_head(q23), spec],
                out_specs=[per_head(own)] * 2 + [whole(msg)],
                out_shape=[own, own, msg],
                compiler_params=params(),
                cost_estimate=cost(per * 3 * 2**27, 4 * 2**20),
                name="level%d" % level,
            )(offsets, qt, kt, vt, q23, before)
            levels.append((o, s, lax.ppermute(m, "ctx", swap)))
        (o2, s2, m2), (o3, s3, m3) = levels
        dest = shape(rows_here // 4, per * DH)
        pieces.append(
            pl.pallas_call(
                functools.partial(merge_kernel, first),
                grid=(per,),
                in_specs=[SMEM]
                + [per_head(x) for x in (o0, s0, o2, s2, o3, s3)]
                + [whole(x) for x in (m1, m2, m3)],
                out_specs=[pl.BlockSpec((rows_here // 4, DH), lambda h: (0, h))] * 4,
                out_shape=[dest] * 4,
                scratch_shapes=[pltpu.VMEM((blocks, RES, SUB, DH), F32)] * 2,
                compiler_params=params(),
                cost_estimate=cost(2**28, 10 * 2**20),
                name="merge",
            )(offsets, o0, s0, o2, s2, o3, s3, m1, m2, m3)
        )
    if GROUPS == 1:
        parts = list(pieces[0])
        for t in range(1, 4):
            parts[t] = lax.ppermute(parts[t], "head", [(i, i ^ t) for i in range(4)])
    model = out_weight.shape[1]
    tile = 512
    return pl.pallas_call(
        project_kernel,
        grid=(model // tile,),
        in_specs=[whole(parts[0])] * 4
        + [pl.BlockSpec((out_weight.shape[0], tile), lambda n: (0, n))],
        out_specs=pl.BlockSpec((rows_here // 4, tile), lambda n: (0, n)),
        out_shape=shape(rows_here // 4, model),
        scratch_shapes=[pltpu.VMEM((rows_here // 4, out_weight.shape[0]), BF16)],
        compiler_params=params(),
        cost_estimate=cost(rows_here // 4 * 2048 * 2048, 12 * 2**20),
        name="project",
    )(*parts, out_weight)


def solution(mesh):
    placed = (P("ctx", "head"), P("ctx", "head"), P("ctx", "head"), P(), P())
    return jax.shard_map(
        body, mesh=mesh, in_specs=placed, out_specs=P(("ctx", "head"), None), check_vma=False
    )
```

```python
import functools
import math

import jax
import jax.numpy as jnp
from jax import lax
from jax.experimental import pallas as pl
from jax.experimental.pallas import tpu as pltpu
from jax.sharding import PartitionSpec as P

DH = 128
HEADS_HERE = 4
PER = 2
RES = 8
SUB = 16
BLK = RES * SUB
NEG = -1e30
RATE = math.log2(math.e) / math.sqrt(DH)
BF16 = jnp.bfloat16
F32 = jnp.float32
VMEM_LIMIT = 20 * 1024 * 1024


def iota(shape, dim):
    return lax.broadcasted_iota(jnp.int32, shape, dim)


def regroup_matrix(inverse):
    row, col = iota((BLK, BLK), 0), iota((BLK, BLK), 1)
    if inverse:
        hit = col == (row % RES) * SUB + row // RES
    else:
        hit = col == (row % SUB) * RES + row // SUB
    return jnp.where(hit, 1.0, 0.0).astype(BF16)


def causal_bias(position, size):
    rows = position(iota((size, size), 0))
    cols = position(iota((size, size), 1))
    return jnp.where(cols <= rows, 0.0, NEG)


def scores_of(q, blocks):
    scores = []
    for k, _, bias in blocks:
        s = lax.dot_general(q, k, (((1,), (1,)), ((), ())), preferred_element_type=F32)
        scores.append(s if bias is None else s + bias)
    return scores


def finish(scores, blocks):
    wide = scores[0]
    for s in scores[1:]:
        wide = jnp.maximum(wide, s)
    top = jnp.max(wide, axis=1, keepdims=True)
    total = None
    for s, (_, v, _) in zip(scores, blocks):
        p = jnp.exp2((s - top) * RATE).astype(BF16)
        with_ones = jnp.concatenate([v, jnp.ones(v.shape, BF16)], axis=1)
        part = jnp.dot(p, with_ones, preferred_element_type=F32)
        total = part if total is None else total + part
    row_sum = total[:, DH:]
    return total[:, :DH] / row_sum, top * RATE + jnp.log2(row_sum)


def attend_all(tasks):
    held = None
    for load, blocks, put in tasks:
        blocks = blocks()
        scores = scores_of(load(), blocks)
        if held is not None:
            held[2](*finish(held[0], held[1]))
        held = (scores, blocks, put)
    held[2](*finish(held[0], held[1]))


def merge(parts):
    top = parts[0][1]
    for _, lse in parts[1:]:
        top = jnp.maximum(top, lse)
    out, weight = 0.0, 0.0
    for o, lse in parts:
        w = jnp.exp2(lse - top)
        out += o * w
        weight += w
    return out / weight, top + jnp.log2(weight)


def rows_of(ref, level, shift, first=0, count=None):
    count = ref.shape[0] - first if count is None else count
    return [
        ref[pl.ds(first, count), shift + j * 2**level].reshape(count * SUB, DH)
        for j in range(RES // 2**level)
    ]


def shift_of(off_ref, level, head):
    return off_ref[level - 1, lax.axis_index("head") * HEADS_HERE + head]


def prep_kernel(off_ref, q_hbm, k_hbm, v_hbm, qt, kt, vt, first, q23, kv2a, kv2b, kv3, held, sems):
    heads, blocks = qt.shape[:2]
    parts = 2
    rows = held.shape[1] // parts
    copies = {}
    for i, src in enumerate((k_hbm, q_hbm, v_hbm)):
        for n in range(parts):
            at = pl.ds(n * rows, rows)
            copies[i, n] = pltpu.make_async_copy(src.at[at], held.at[i, at], sems.at[i, n])
            copies[i, n].start()
    turn = regroup_matrix(False)
    for i, dst in enumerate((kt, qt, vt)):
        for n in range(parts):
            copies[i, n].wait()
            for b in range(n * blocks // parts, (n + 1) * blocks // parts):
                x = held[i, b * BLK : (b + 1) * BLK, :]
                x = jnp.dot(turn, x, preferred_element_type=F32).astype(BF16)
                for h in range(heads):
                    dst[h, b] = x[:, h * DH : (h + 1) * DH].reshape(RES, SUB, DH)
    for h in range(heads):
        o2, o3 = (shift_of(off_ref, level, h) for level in (2, 3))
        g, n = divmod(h, PER)
        for j, x in enumerate(rows_of(qt.at[h], 2, o2) + rows_of(qt.at[h], 3, o3)):
            q23[h, j] = x
        for i, src in enumerate((kt, vt)):
            for j, x in enumerate(rows_of(src.at[h], 2, o2)):
                (kv2a, kv2b)[g][n, i, j] = x
            kv3[h, i] = rows_of(src.at[h], 3, o3)[0]

    @pl.when(lax.axis_index("ctx") % 2 == 1)
    def _():
        for h in range(2):
            for j, x in enumerate(rows_of(qt.at[h], 1, shift_of(off_ref, 1, h))):
                first[4 * h + j] = x

    @pl.when(lax.axis_index("ctx") % 2 == 0)
    def _():
        for i, src in enumerate((kt, vt)):
            for j, x in enumerate(rows_of(src.at[3], 1, shift_of(off_ref, 1, 3))):
                first[4 * i + j] = x


def own_kernel(group, off_ref, qt, kt, vt, token, out, lse):
    blocks = qt.shape[1]
    tasks = []

    def level0(h, n, step):
        head = group * PER + h
        size = step * BLK
        bias = causal_bias(lambda r: r // BLK * BLK + r % SUB * RES + r % BLK // SUB, size)
        load = lambda ref, n: ref[head, n * step : (n + 1) * step].reshape(size, DH)

        def put(o, s):
            out[h, n * step : (n + 1) * step] = o.reshape(step, RES, SUB, DH)
            lse[h, n * step : (n + 1) * step] = s.reshape(step, RES, SUB, DH)

        tasks.append(
            (
                lambda: load(qt, n),
                lambda: [
                    (load(kt, i), load(vt, i), bias if i == n else None) for i in range(n + 1)
                ],
                put,
            )
        )

    def level1(h, n, step):
        head = group * PER + h
        shift = shift_of(off_ref, 1, head)
        rows = step * SUB
        slices = RES // 2
        size = rows * slices
        bias = causal_bias(lambda r: r % rows * slices + r // rows, size)

        def load(ref, n):
            return jnp.concatenate(rows_of(ref.at[head], 1, shift, n * step, step), axis=0)

        def put(o, s):
            for j in range(slices):
                at = (h, pl.ds(n * step, step), shift + 2 * j)
                was = (out[at].reshape(rows, DH), lse[at].reshape(rows, DH))
                fresh = (o[j * rows : (j + 1) * rows], s[j * rows : (j + 1) * rows])
                both, total = merge([was, fresh])
                out[at] = both.reshape(step, SUB, DH)
                lse[at] = total.reshape(step, SUB, DH)

        tasks.append(
            (
                lambda: load(qt, n),
                lambda: [
                    (load(kt, i), load(vt, i), bias if i == n else None) for i in range(n + 1)
                ],
                put,
            )
        )

    for n in range(blocks // 2):
        for h in range(PER):
            level0(h, n, 2)
    for n in range(blocks // 4):
        for h in range(PER):
            level1(h, n, 4)
    attend_all(tasks)


def put_stat(slab, stat, place):
    lane = iota(stat.shape, 1)
    rest = stat
    now = slab[...]
    for i in range(3):
        piece = rest.astype(BF16)
        rest = rest - piece.astype(F32)
        now = jnp.where(lane == place + 32 * i, piece, now)
    slab[...] = now


def get_stat(slab, place):
    lane = iota(slab.shape, 1)
    hit = (lane == place) | (lane == place + 32) | (lane == place + 64)
    return jnp.sum(jnp.where(hit, slab[...].astype(F32), 0.0), axis=1, keepdims=True)


def put_message(msg, place, o, s, count):
    rows = msg.shape[1]
    for j in range(count):
        at = slice(j * rows, (j + 1) * rows)
        msg[place + j] = o[at].astype(BF16)
        put_stat(msg.at[msg.shape[0] - 1], s[at], place + j)


def pair_tasks(off_ref, head, load, keys, values, put):
    count = RES // 2

    def blocks():
        k, v = keys(), values()
        return [
            (jnp.concatenate(k[i : i + 2], axis=0), jnp.concatenate(v[i : i + 2], axis=0), None)
            for i in range(0, count, 2)
        ]

    return [
        (
            lambda j=j: jnp.concatenate(load()[j : j + 2], axis=0),
            blocks,
            lambda o, s, j=j: put(j, o, s),
        )
        for j in range(0, count, 2)
    ]


def lower_kernel(heads, off_ref, got, qt, kt, vt, token, msg, *local):
    last = msg.shape[0] - 1
    count = RES // 2
    rows = msg.shape[1]
    later = lax.axis_index("ctx") % 2 == 1
    msg[...] = jnp.zeros(msg.shape, BF16)

    @pl.when(jnp.logical_not(later))
    def _():
        tasks = []
        for n, head in enumerate(heads):
            shift = shift_of(off_ref, 1, head)
            tasks += pair_tasks(
                off_ref,
                head,
                lambda n=n: [got[n * count + j] for j in range(count)],
                lambda head=head, shift=shift: rows_of(kt.at[head], 1, shift),
                lambda head=head, shift=shift: rows_of(vt.at[head], 1, shift),
                lambda j, o, s, n=n: put_message(msg, n * count + j, o, s, 2),
            )
        attend_all(tasks)
        for ref, fill in zip(local, (0.0, NEG)):
            ref[...] = jnp.full(ref.shape, fill, F32)

    if not local:
        return

    @pl.when(later)
    def _():
        for j, x in enumerate(rows_of(qt.at[2], 1, shift_of(off_ref, 1, 2))):
            msg[j] = x
        shift = shift_of(off_ref, 1, 3)

        def put(j, o, s):
            for i in range(2):
                local[0][j + i] = o[i * rows : (i + 1) * rows]
                local[1][j + i] = s[i * rows : (i + 1) * rows]

        attend_all(
            pair_tasks(
                off_ref,
                3,
                lambda: rows_of(qt.at[3], 1, shift),
                lambda: [got[j] for j in range(count)],
                lambda: [got[count + j] for j in range(count)],
                put,
            )
        )


def levels_kernel(group, levels, partner, off_ref, qt, kt, vt, q23, *rest):
    token, rest = rest[0], rest[1:]
    before, outs = {}, {}
    for level in levels:
        number = 1 if level == 2 else 2
        before[level], rest = rest[:number], rest[number:]
    if partner:
        (msg,) = rest
        msg[msg.shape[0] - 1] = jnp.zeros(msg.shape[1:], BF16)
    else:
        for level in levels:
            outs[level], rest = rest[:2], rest[2:]
    ctx = lax.axis_index("ctx")
    z = ctx // 2
    rows = q23.shape[2]
    tasks = []
    place = 0
    for level in levels:
        count = RES // 2**level
        size = count * rows
        base = 0 if level == 2 else 2
        triangle = causal_bias(lambda r, c=count: r % rows * c + r // rows, size)
        later = jnp.where(ctx % 2 == 0, 0.0, NEG)
        for h in range(PER):
            head = group * PER + h
            shift = shift_of(off_ref, level, head)

            def whole(ref, head=head, shift=shift, level=level):
                return jnp.concatenate(rows_of(ref.at[head], level, shift), axis=0)

            def past(h=h, head=head, level=level, size=size):
                if level == 2:
                    kv = before[2][0]
                    bias = jnp.where(z % 2 == 1, 0.0, NEG)
                    return [(kv[h, 0].reshape(size, DH), kv[h, 1].reshape(size, DH), bias)]
                near, far = before[3]
                odd = jnp.where(z % 2 == 1, 0.0, NEG)
                high = jnp.where(z % 4 >= 2, 0.0, NEG)
                return [
                    (near[head, 0], near[head, 1], odd),
                    (far[0, h, 0], far[0, h, 1], high),
                    (far[1, h, 0], far[1, h, 1], high),
                ]

            def own(o, s, h=h, count=count, level=level):
                for j in range(count):
                    at = slice(j * rows, (j + 1) * rows)
                    outs[level][0][h, j] = o[at]
                    outs[level][1][h, j] = s[at]

            if partner:
                load = lambda h=head, b=base, c=count, n=size: q23[h, b : b + c].reshape(n, DH)
                put = lambda o, s, p=place, c=count: put_message(msg, p, o, s, c)
                bias = later
            else:
                load = lambda whole=whole: whole(qt)
                put = own
                bias = triangle
            tasks.append(
                (
                    load,
                    lambda whole=whole, past=past, b=bias: past() + [(whole(kt), whole(vt), b)],
                    put,
                )
            )
            place += count
    attend_all(tasks)


def merge_kernel(group, off_ref, o0, s0, o2, s2, o3, s3, m1, m23, *rest):
    if group:
        o1, s1, *rest = rest
    token, d0, d1, d2, d3, acc, sums = rest
    ctx = lax.axis_index("ctx")
    blocks = o0.shape[1]
    rows = blocks * SUB
    for h in range(PER):
        for level in (1, 2, 3):
            shift = shift_of(off_ref, level, group * PER + h)
            count = RES // 2**level
            msg = m1 if level == 1 else m23
            for j in range(count):
                at = (h, slice(None), shift + j * 2**level)
                place = h * count + j + (2 * PER if level == 3 else 0)
                parts = [(acc[at].reshape(rows, DH), sums[at].reshape(rows, DH))]
                if level == 1 and group and h:
                    parts.append((o1[j], s1[j]))
                else:
                    stat = get_stat(msg.at[msg.shape[0] - 1], place)
                    if level == 1:
                        stat = jnp.where(ctx % 2 == 1, stat, NEG)
                    parts.append((msg[place].astype(F32), jnp.broadcast_to(stat, (rows, DH))))
                if level > 1:
                    own = (o2, s2) if level == 2 else (o3, s3)
                    parts.append((own[0][h, j], own[1][h, j]))
                o, s = merge(parts)
                acc[at] = o.reshape(blocks, SUB, DH)
                sums[at] = s.reshape(blocks, SUB, DH)
    mine = lax.axis_index("head")
    per = blocks // 4
    for t, dest in enumerate((d0, d1, d2, d3)):
        for h in range(PER):
            x = acc[h, pl.ds((mine ^ t) * per, per)].reshape(per * BLK, DH)
            dest[:, h * DH : (h + 1) * DH] = x.astype(BF16)


def project_kernel(group, a0, a1, a2, a3, w_ref, *rest):
    *before, out, plain = rest
    width = a0.shape[1]
    stride = HEADS_HERE * DH
    back = regroup_matrix(True)
    for t, src in enumerate((a0, a1, a2, a3)):
        for b in range(src.shape[0] // BLK):
            at = slice(b * BLK, (b + 1) * BLK)
            x = jnp.dot(back, src[at, :], preferred_element_type=F32)
            plain[at, t * width : (t + 1) * width] = x.astype(BF16)
    mine = lax.axis_index("head")
    tile = 512

    @pl.loop(0, out.shape[1] // tile)
    def _(n):
        cols = pl.ds(pl.multiple_of(n * tile, tile), tile)
        total = before[0][:, cols] if group else None
        for t in range(4):
            first = pl.multiple_of((mine ^ t) * stride + group * width, width)
            part = jnp.dot(
                plain[:, t * width : (t + 1) * width],
                w_ref[pl.ds(first, width), cols],
                preferred_element_type=F32,
            )
            total = part if total is None else total + part
        out[:, cols] = total.astype(out.dtype)


SMEM = pl.BlockSpec(memory_space=pltpu.SMEM)
VMEM = pl.BlockSpec(memory_space=pltpu.VMEM)
ANY = pl.BlockSpec(memory_space=pl.ANY)
HBM = pl.BlockSpec(memory_space=pltpu.HBM)


def shape(*dims, dtype=BF16):
    return jax.ShapeDtypeStruct(dims, dtype)


def call(kernel, specs, outs, name, macs, moved=4 * 2**20, scratch=(), aliases={}):
    return pl.pallas_call(
        kernel,
        in_specs=specs,
        out_specs=jax.tree.map(lambda _: VMEM, outs),
        out_shape=outs,
        scratch_shapes=scratch,
        input_output_aliases=aliases,
        compiler_params=pltpu.CompilerParams(vmem_limit_bytes=VMEM_LIMIT),
        cost_estimate=pl.CostEstimate(
            flops=int(2 * macs), bytes_accessed=moved, transcendentals=0
        ),
        name=name,
    )


def body(queries, keys, values, offsets, out_weight):
    rows_here, width = queries.shape
    blocks = rows_here // BLK
    heads = width // DH
    slots = rows_here // RES
    piece = (slots, DH)
    regrouped = shape(heads, blocks, RES, SUB, DH)
    ctx_size = lax.axis_size("ctx")
    swap = [(i, i ^ 1) for i in range(ctx_size)]
    down = [(i + 1, i) for i in range(0, ctx_size, 2)]
    up = [(i, i + 1) for i in range(0, ctx_size, 2)]
    near = [(i, i ^ 2) for i in range(ctx_size)]
    even = [(i, i + 2) for i in range(ctx_size) if i & 2 == 0]
    far = [(i, i + 4) for i in range(ctx_size) if i & 4 == 0]
    over = [[(i, i ^ t) for i in range(4)] for t in range(4)]

    qt, kt, vt, first, q23, kv2a, kv2b, kv3 = call(
        prep_kernel,
        [SMEM, HBM, HBM, HBM],
        [
            regrouped,
            regrouped,
            regrouped,
            shape(8, *piece),
            shape(heads, 3, *piece),
            shape(PER, 2, 2, *piece),
            shape(PER, 2, 2, *piece),
            shape(heads, 2, *piece),
        ],
        "prep",
        2**30,
        scratch=[pltpu.VMEM((3, rows_here, width), BF16), pltpu.SemaphoreType.DMA((3, 2))],
    )(offsets, queries, keys, values)

    def own(group, token):
        part = shape(PER, blocks, RES, SUB, DH, dtype=F32)
        return call(
            functools.partial(own_kernel, group),
            [SMEM, VMEM, VMEM, VMEM, ANY],
            [part, part],
            "own%d" % group,
            5 * 2**30,
        )(offsets, qt, kt, vt, token)

    def lower(which, got, token):
        outs = [shape(len(which) * 4 + 1, *piece)]
        if len(which) == 2:
            outs += [shape(4, *piece, dtype=F32)] * 2
        return call(
            functools.partial(lower_kernel, which),
            [SMEM] + [VMEM] * 4 + [ANY],
            outs,
            "lower%d" % which[0],
            1.5 * 2**30,
        )(offsets, got, qt, kt, vt, token)

    def levels(group, partner, before, token):
        if partner:
            outs = [shape(PER * 3 + 1, *piece)]
        else:
            outs = [shape(PER, 2, *piece, dtype=F32)] * 2 + [shape(PER, 1, *piece, dtype=F32)] * 2
        return call(
            functools.partial(levels_kernel, group, (2, 3), partner),
            [SMEM] + [VMEM] * 4 + [ANY] + [VMEM] * len(before),
            outs,
            ("partner%d" if partner else "mine%d") % group,
            1.5 * 2**30,
        )(offsets, qt, kt, vt, q23, token, *before)

    def merged(group, parts, token):
        part = shape(PER, blocks, RES, SUB, DH, dtype=F32)
        dest = shape(rows_here // 4, PER * DH)
        return call(
            functools.partial(merge_kernel, group),
            [SMEM] + [VMEM] * len(parts) + [ANY],
            [dest] * 4 + [part] * 2,
            "merge%d" % group,
            2**29,
            aliases={1: 4, 2: 5},
        )(offsets, *parts, token)[:4]

    def spread(rows):
        return [rows[0]] + [lax.ppermute(rows[t], "head", over[t]) for t in (1, 2, 3)]

    def both(group):
        cut = slice(group * PER, (group + 1) * PER)
        return jnp.stack([kv3[cut], kv3_near[cut]])

    kv3_near = lax.ppermute(kv3, "ctx", near)
    first = lax.ppermute(first, "ctx", swap)
    q23 = lax.ppermute(q23, "ctx", swap)
    o0a, s0a = own(0, kv3)
    far_a = both(0)
    kv2a, far_a = lax.optimization_barrier((kv2a, far_a))
    o0b, s0b = own(1, far_a)
    far_a = lax.ppermute(far_a, "ctx", far)
    kv2a = lax.ppermute(kv2a, "ctx", even)
    msg1a, o1, s1 = lower((0, 1), first, s0b)
    turn = lax.ppermute(msg1a, "ctx", swap)
    before_a = [kv2a, kv3_near, far_a]
    (msg_a,) = levels(0, True, before_a, msg1a)
    got_a = lax.ppermute(msg_a, "ctx", swap)
    far_b, kv2b, msg_a = lax.optimization_barrier((both(1), kv2b, msg_a))
    far_b = lax.ppermute(far_b, "ctx", far)
    kv2b = lax.ppermute(kv2b, "ctx", even)
    (msg1b,) = lower((2,), turn, msg_a)
    got1b = lax.ppermute(msg1b, "ctx", up)
    mine_a = levels(0, False, before_a, msg1b)
    rows_a = merged(0, (o0a, s0a, *mine_a, turn, got_a), mine_a[0])
    rows_a_all = spread(rows_a)
    before_b = [kv2b, kv3_near, far_b]
    (msg_b,) = levels(1, True, before_b, rows_a[0])
    got_b = lax.ppermute(msg_b, "ctx", swap)
    mine_b = levels(1, False, before_b, msg_b)
    model = out_weight.shape[1]
    plain = [pltpu.VMEM((rows_here // 4, 4 * PER * DH), BF16)]
    half = call(
        functools.partial(project_kernel, 0),
        [VMEM] * 5 + [ANY],
        shape(rows_here // 4, model, dtype=F32),
        "project0",
        2**30,
        scratch=plain,
    )(*rows_a_all, out_weight, mine_b[0])
    rows_b = merged(1, (o0b, s0b, *mine_b, got1b, got_b, o1, s1), half)
    rows_b_all = spread(rows_b)
    return call(
        functools.partial(project_kernel, 1),
        [VMEM] * 6,
        shape(rows_here // 4, model),
        "project1",
        2**30,
        scratch=plain,
    )(*rows_b_all, out_weight, half)


def solution(mesh):
    placed = (P("ctx", "head"), P("ctx", "head"), P("ctx", "head"), P(), P())
    return jax.shard_map(
        body, mesh=mesh, in_specs=placed, out_specs=P(("ctx", "head"), None), check_vma=False
    )
```

```python
import functools
import math

import jax
import jax.numpy as jnp
from jax import lax
from jax.experimental import pallas as pl
from jax.experimental.pallas import tpu as pltpu
from jax.sharding import PartitionSpec as P

DH = 128
HEADS_HERE = 4
GROUPS = ((0, 1), (2,), (3,))
RES = 8
SUB = 16
BLK = RES * SUB
NEG = -1e30
RATE = math.log2(math.e) / math.sqrt(DH)
BF16 = jnp.bfloat16
F32 = jnp.float32
VMEM_LIMIT = 20 * 1024 * 1024


COST = {'mine0': 10**10}


def iota(shape, dim):
    return lax.broadcasted_iota(jnp.int32, shape, dim)


def regroup_matrix(inverse):
    row, col = iota((BLK, BLK), 0), iota((BLK, BLK), 1)
    if inverse:
        hit = col == (row % RES) * SUB + row // RES
    else:
        hit = col == (row % SUB) * RES + row // SUB
    return jnp.where(hit, 1.0, 0.0).astype(BF16)


def causal_bias(position, size):
    rows = position(iota((size, size), 0))
    cols = position(iota((size, size), 1))
    return jnp.where(cols <= rows, 0.0, NEG)


def scores_of(q, blocks):
    scores = []
    for k, _, bias in blocks:
        s = lax.dot_general(q, k, (((1,), (1,)), ((), ())), preferred_element_type=F32)
        scores.append(s if bias is None else s + bias)
    return scores


def finish(scores, blocks):
    wide = scores[0]
    for s in scores[1:]:
        wide = jnp.maximum(wide, s)
    top = jnp.max(wide, axis=1, keepdims=True)
    total = None
    for s, (_, v, _) in zip(scores, blocks):
        p = jnp.exp2((s - top) * RATE).astype(BF16)
        with_ones = jnp.concatenate([v, jnp.ones(v.shape, BF16)], axis=1)
        part = jnp.dot(p, with_ones, preferred_element_type=F32)
        total = part if total is None else total + part
    row_sum = total[:, DH:]
    return total[:, :DH] / row_sum, top * RATE + jnp.log2(row_sum)


def attend_all(tasks):
    held = None
    for load, blocks, put in tasks:
        blocks = blocks()
        scores = scores_of(load(), blocks)
        if held is not None:
            held[2](*finish(held[0], held[1]))
        held = (scores, blocks, put)
    held[2](*finish(held[0], held[1]))


def merge(parts):
    top = parts[0][1]
    for _, lse in parts[1:]:
        top = jnp.maximum(top, lse)
    out, weight = 0.0, 0.0
    for o, lse in parts:
        w = jnp.exp2(lse - top)
        out += o * w
        weight += w
    return out / weight, top + jnp.log2(weight)


def add_rows(out, lse, at, part):
    held = out[at].shape
    was = (out[at].reshape(part[0].shape), lse[at].reshape(part[0].shape))
    o, s = merge([was, part])
    out[at] = o.reshape(held)
    lse[at] = s.reshape(held)


def rows_of(ref, level, shift, first=0, count=None):
    count = ref.shape[0] - first if count is None else count
    return [
        ref[pl.ds(first, count), shift + j * 2**level].reshape(count * SUB, DH)
        for j in range(RES // 2**level)
    ]


def shift_of(off_ref, level, head):
    return off_ref[level - 1, lax.axis_index("head") * HEADS_HERE + head]


def regroup(sources, targets):
    turn = regroup_matrix(False)
    heads, blocks = targets[0].shape[:2]
    for src, dst in zip(sources, targets):
        for b in range(blocks):
            x = src[b * BLK : (b + 1) * BLK, :]
            x = jnp.dot(turn, x, preferred_element_type=F32).astype(BF16)
            for h in range(heads):
                dst[h, b] = x[:, h * DH : (h + 1) * DH].reshape(RES, SUB, DH)


def prep_kv_kernel(off_ref, k_ref, v_ref, kt, vt, kv3, *kv2):
    regroup((k_ref, v_ref), (kt, vt))
    for h in range(kt.shape[0]):
        o2, o3 = (shift_of(off_ref, level, h) for level in (2, 3))
        (g,) = [g for g, members in enumerate(GROUPS) if h in members]
        n = GROUPS[g].index(h)
        for i, src in enumerate((kt, vt)):
            for j, x in enumerate(rows_of(src.at[h], 2, o2)):
                kv2[g][n, i, j] = x
            kv3[h, i] = rows_of(src.at[h], 3, o3)[0]


def prep_q_kernel(off_ref, q_ref, kt, vt, qt, first, q23):
    regroup((q_ref,), (qt,))
    for h in range(qt.shape[0]):
        o2, o3 = (shift_of(off_ref, level, h) for level in (2, 3))
        for j, x in enumerate(rows_of(qt.at[h], 2, o2) + rows_of(qt.at[h], 3, o3)):
            q23[h, j] = x

    @pl.when(lax.axis_index("ctx") % 2 == 1)
    def _():
        for h in range(2):
            for j, x in enumerate(rows_of(qt.at[h], 1, shift_of(off_ref, 1, h))):
                first[4 * h + j] = x

    @pl.when(lax.axis_index("ctx") % 2 == 0)
    def _():
        for i, src in enumerate((kt, vt)):
            for j, x in enumerate(rows_of(src.at[3], 1, shift_of(off_ref, 1, 3))):
                first[4 * i + j] = x


def own_kernel(heads, off_ref, qt, kt, vt, token, *outs):
    blocks = qt.shape[1]
    tasks = []

    def level0(h, n, step):
        head, out, lse = heads[h], outs[2 * h], outs[2 * h + 1]
        size = step * BLK
        bias = causal_bias(lambda r: r // BLK * BLK + r % SUB * RES + r % BLK // SUB, size)
        load = lambda ref, n: ref[head, n * step : (n + 1) * step].reshape(size, DH)

        def put(o, s):
            out[n * step : (n + 1) * step] = o.reshape(step, RES, SUB, DH)
            lse[n * step : (n + 1) * step] = s.reshape(step, RES, SUB, DH)

        tasks.append(
            (
                lambda: load(qt, n),
                lambda: [
                    (load(kt, i), load(vt, i), bias if i == n else None) for i in range(n + 1)
                ],
                put,
            )
        )

    def level1(h, n, step):
        head, out, lse = heads[h], outs[2 * h], outs[2 * h + 1]
        shift = shift_of(off_ref, 1, head)
        rows = step * SUB
        slices = RES // 2
        size = rows * slices
        bias = causal_bias(lambda r: r % rows * slices + r // rows, size)

        def load(ref, n):
            return jnp.concatenate(rows_of(ref.at[head], 1, shift, n * step, step), axis=0)

        def put(o, s):
            for j in range(slices):
                at = (pl.ds(n * step, step), shift + 2 * j)
                fresh = (o[j * rows : (j + 1) * rows], s[j * rows : (j + 1) * rows])
                add_rows(out, lse, at, fresh)

        tasks.append(
            (
                lambda: load(qt, n),
                lambda: [
                    (load(kt, i), load(vt, i), bias if i == n else None) for i in range(n + 1)
                ],
                put,
            )
        )

    for n in range(blocks // 2):
        for h in range(len(heads)):
            level0(h, n, 2)
    for n in range(blocks // 4):
        for h in range(len(heads)):
            level1(h, n, 4)
    attend_all(tasks)


def put_stat(slab, stat, place):
    lane = iota(stat.shape, 1)
    rest = stat
    now = slab[...]
    for i in range(3):
        piece = rest.astype(BF16)
        rest = rest - piece.astype(F32)
        now = jnp.where(lane == place + 32 * i, piece, now)
    slab[...] = now


def get_stat(slab, place):
    lane = iota(slab.shape, 1)
    hit = (lane == place) | (lane == place + 32) | (lane == place + 64)
    return jnp.sum(jnp.where(hit, slab[...].astype(F32), 0.0), axis=1, keepdims=True)


def put_message(msg, place, o, s, count):
    rows = msg.shape[1]
    for j in range(count):
        at = slice(j * rows, (j + 1) * rows)
        msg[place + j] = o[at].astype(BF16)
        put_stat(msg.at[msg.shape[0] - 1], s[at], place + j)


def pair_tasks(load, keys, values, put):
    count = RES // 2

    def blocks():
        k, v = keys(), values()
        return [
            (jnp.concatenate(k[i : i + 2], axis=0), jnp.concatenate(v[i : i + 2], axis=0), None)
            for i in range(0, count, 2)
        ]

    return [
        (
            lambda j=j: jnp.concatenate(load()[j : j + 2], axis=0),
            blocks,
            lambda o, s, j=j: put(j, o, s),
        )
        for j in range(0, count, 2)
    ]


def lower_kernel(heads, off_ref, got, qt, kt, vt, token, msg, *local):
    last = msg.shape[0] - 1
    count = RES // 2
    rows = msg.shape[1]
    later = lax.axis_index("ctx") % 2 == 1
    msg[...] = jnp.zeros(msg.shape, BF16)

    @pl.when(jnp.logical_not(later))
    def _():
        tasks = []
        for n, head in enumerate(heads):
            shift = shift_of(off_ref, 1, head)
            tasks += pair_tasks(
                lambda n=n: [got[n * count + j] for j in range(count)],
                lambda head=head, shift=shift: rows_of(kt.at[head], 1, shift),
                lambda head=head, shift=shift: rows_of(vt.at[head], 1, shift),
                lambda j, o, s, n=n: put_message(msg, n * count + j, o, s, 2),
            )
        attend_all(tasks)
        for ref, fill in zip(local, (0.0, NEG)):
            ref[...] = jnp.full(ref.shape, fill, F32)

    @pl.when(later)
    def _():
        for j, x in enumerate(rows_of(qt.at[2], 1, shift_of(off_ref, 1, 2))):
            msg[j] = x
        shift = shift_of(off_ref, 1, 3)

        def put(j, o, s):
            for i in range(2):
                local[0][j + i] = o[i * rows : (i + 1) * rows]
                local[1][j + i] = s[i * rows : (i + 1) * rows]

        attend_all(
            pair_tasks(
                lambda: rows_of(qt.at[3], 1, shift),
                lambda: [got[j] for j in range(count)],
                lambda: [got[count + j] for j in range(count)],
                put,
            )
        )


def level_blocks(off_ref, level, head, n, q23, kt, vt, kv2, near, far):
    ctx = lax.axis_index("ctx")
    z = ctx // 2
    shift = shift_of(off_ref, level, head)
    count = RES // 2**level
    rows = q23.shape[2]
    size = count * rows
    odd = jnp.where(z % 2 == 1, 0.0, NEG)
    high = jnp.where(z % 4 >= 2, 0.0, NEG)

    def whole(ref):
        return jnp.concatenate(rows_of(ref.at[head], level, shift), axis=0)

    def blocks(bias):
        if level == 2:
            past = [(kv2[n, 0].reshape(size, DH), kv2[n, 1].reshape(size, DH), odd)]
        else:
            past = [
                (near[head, 0], near[head, 1], odd),
                (far[0, n, 0], far[0, n, 1], high),
                (far[1, n, 0], far[1, n, 1], high),
            ]
        return past + [(whole(kt), whole(vt), bias)]

    return whole, blocks, shift, count, rows


def partner_kernel(heads, extra, off_ref, kt, vt, q23, kv2, near, far, token, *refs):
    *turn, msg = refs
    later = jnp.where(lax.axis_index("ctx") % 2 == 0, 0.0, NEG)
    msg[msg.shape[0] - 1] = jnp.zeros(msg.shape[1:], BF16)
    tasks, place = [], 0
    for level in (2, 3):
        for n, head in enumerate(heads):
            _, blocks, _, count, rows = level_blocks(
                off_ref, level, head, n, q23, kt, vt, kv2, near, far
            )
            first = 0 if level == 2 else 2
            tasks.append(
                (
                    lambda h=head, f=first, c=count, r=rows: q23[h, f : f + c].reshape(c * r, DH),
                    lambda blocks=blocks: blocks(later),
                    lambda o, s, p=place, c=count: put_message(msg, p, o, s, c),
                )
            )
            place += count
    for head in extra:
        shift = shift_of(off_ref, 1, head)
        tasks += pair_tasks(
            lambda: [turn[0][j] for j in range(RES // 2)],
            lambda shift=shift, head=head: rows_of(kt.at[head], 1, shift),
            lambda shift=shift, head=head: rows_of(vt.at[head], 1, shift),
            lambda j, o, s, p=place: put_message(msg, p + j, o, s, 2),
        )
    attend_all(tasks)


def add_lower(off_ref, head, msg, first, out, lse):
    later = lax.axis_index("ctx") % 2 == 1
    for j in range(RES // 2):
        at = (slice(None), shift_of(off_ref, 1, head) + 2 * j)
        stat = jnp.where(later, get_stat(msg.at[msg.shape[0] - 1], first + j), NEG)
        part = msg[first + j].astype(F32)
        add_rows(out, lse, at, (part, jnp.broadcast_to(stat, part.shape)))


def mine_kernel(heads, off_ref, *refs):
    number = len(heads)
    refs = refs[2 * number :]
    (qt, kt, vt, q23, kv2, near, far, token), refs = refs[:8], refs[8:]
    lower, state = refs[: -2 * number], refs[-2 * number :]
    tasks = []
    for level in (2, 3):
        for n, head in enumerate(heads):
            out, lse = state[2 * n : 2 * n + 2]
            whole, blocks, shift, count, rows = level_blocks(
                off_ref, level, head, n, q23, kt, vt, kv2, near, far
            )
            triangle = causal_bias(lambda r, c=count, m=rows: r % m * c + r // m, count * rows)

            def put(o, s, out=out, lse=lse, shift=shift, level=level, count=count, rows=rows):
                for j in range(count):
                    at = slice(j * rows, (j + 1) * rows)
                    add_rows(out, lse, (slice(None), shift + j * 2**level), (o[at], s[at]))

            tasks.append(
                (
                    lambda whole=whole: whole(qt),
                    lambda blocks=blocks, t=triangle: blocks(t),
                    put,
                )
            )
    attend_all(tasks)
    for n, head in enumerate(heads):
        if len(lower) == 1:
            add_lower(off_ref, head, lower[0], n * (RES // 2), state[2 * n], state[2 * n + 1])
        elif lower:
            for j in range(RES // 2):
                at = (slice(None), shift_of(off_ref, 1, head) + 2 * j)
                add_rows(state[2 * n], state[2 * n + 1], at, (lower[0][j], lower[1][j]))


def finish_kernel(heads, off_ref, *refs):
    number = len(heads)
    refs = refs[2 * number :]
    msg, token, *extra = refs[: -4 - 2 * number]
    dests, state = refs[-4 - 2 * number : -2 * number], refs[-2 * number :]
    if extra:
        add_lower(off_ref, heads[0], extra[0], 6, *state)
    place = 0
    for level in (2, 3):
        for n, head in enumerate(heads):
            shift = shift_of(off_ref, level, head)
            for j in range(RES // 2**level):
                part = msg[place].astype(F32)
                stat = get_stat(msg.at[msg.shape[0] - 1], place)
                add_rows(
                    state[2 * n],
                    state[2 * n + 1],
                    (slice(None), shift + j * 2**level),
                    (part, jnp.broadcast_to(stat, part.shape)),
                )
                place += 1
    mine = lax.axis_index("head")
    per = state[0].shape[0] // 4
    for t, dest in enumerate(dests):
        for n in range(number):
            x = state[2 * n][pl.ds((mine ^ t) * per, per)].reshape(per * BLK, DH)
            dest[:, n * DH : (n + 1) * DH] = x.astype(BF16)


def weights_kernel(w_ref, token, out):
    mine = lax.axis_index("head")
    at = 0
    for members in GROUPS:
        width = len(members) * DH
        for t in range(4):
            first = (mine ^ t) * (HEADS_HERE * DH) + members[0] * DH
            out[at : at + width, :] = w_ref[pl.ds(pl.multiple_of(first, DH), width), :]
            at += width


def project_kernel(first, added, final, *refs):
    if final:
        *pieces, w_ref, token, out_hbm, plain, out, sems = refs
    else:
        *pieces, w_ref, token, out, plain = refs
    if added:
        *pieces, before = pieces
    back = regroup_matrix(True)
    depth = plain.shape[1]
    for b in range(plain.shape[0] // BLK):
        rows = slice(b * BLK, (b + 1) * BLK)
        x = jnp.concatenate([src[rows, :] for src in pieces], axis=1)
        plain[rows, :] = jnp.dot(back, x, preferred_element_type=F32).astype(BF16)
    tile = 512
    steps = out.shape[1] // tile

    def copy(step):
        cols = pl.ds(pl.multiple_of(step * tile, tile), tile)
        return pltpu.make_async_copy(out.at[:, cols], out_hbm.at[:, cols], sems.at[step])

    @pl.loop(0, steps)
    def _(step):
        cols = pl.ds(pl.multiple_of(step * tile, tile), tile)
        total = jnp.dot(
            plain[...], w_ref[first : first + depth, cols], preferred_element_type=F32
        )
        if added:
            total = total + before[:, cols]
        out[:, cols] = total.astype(out.dtype)
        if final:
            copy(step).start()

    if final:

        @pl.loop(0, steps)
        def _(step):
            copy(step).wait()


SMEM = pl.BlockSpec(memory_space=pltpu.SMEM)
VMEM = pl.BlockSpec(memory_space=pltpu.VMEM)
ANY = pl.BlockSpec(memory_space=pl.ANY)


def shape(*dims, dtype=BF16):
    return jax.ShapeDtypeStruct(dims, dtype)


def call(kernel, specs, outs, name, scratch=(), aliases={}, out_spec=VMEM):
    return pl.pallas_call(
        kernel,
        in_specs=specs,
        out_specs=jax.tree.map(lambda _: out_spec, outs),
        out_shape=outs,
        scratch_shapes=scratch,
        input_output_aliases=aliases,
        compiler_params=pltpu.CompilerParams(vmem_limit_bytes=VMEM_LIMIT),
        cost_estimate=pl.CostEstimate(flops=COST.get(name, 10**9), bytes_accessed=1, transcendentals=0),
        name=name,
    )


def body(queries, keys, values, offsets, out_weight):
    rows_here, width = queries.shape
    blocks = rows_here // BLK
    heads = width // DH
    slots = rows_here // RES
    piece = (slots, DH)
    regrouped = shape(heads, blocks, RES, SUB, DH)
    ctx_size = lax.axis_size("ctx")
    swap = [(i, i ^ 1) for i in range(ctx_size)]
    near = [(i, i ^ 2) for i in range(ctx_size)]
    far = [(i, i ^ 4) for i in range(ctx_size)]
    over = [[(i, i ^ t) for i in range(4)] for t in range(4)]

    kt, vt, kv3, *kv2 = call(
        prep_kv_kernel,
        [SMEM, VMEM, VMEM],
        [regrouped, regrouped, shape(heads, 2, *piece)]
        + [shape(len(members), 2, 2, *piece) for members in GROUPS],
        "prep_kv",
    )(offsets, keys, values)
    kv3_near = lax.ppermute(kv3, "ctx", near)
    qt, first, q23 = call(
        prep_q_kernel,
        [SMEM, VMEM, VMEM, VMEM],
        [regrouped, shape(8, *piece), shape(heads, 3, *piece)],
        "prep_q",
    )(offsets, queries, kt, vt)
    first = lax.ppermute(first, "ctx", swap)
    q23 = lax.ppermute(q23, "ctx", swap)

    state = shape(blocks, RES, SUB, DH, dtype=F32)

    def own(members, token):
        return call(
            functools.partial(own_kernel, members),
            [SMEM, VMEM, VMEM, VMEM, ANY],
            [state] * (2 * len(members)),
            "own%d" % members[0],
        )(offsets, qt, kt, vt, token)

    def lower(members, got, token):
        return call(
            functools.partial(lower_kernel, members),
            [SMEM] + [VMEM] * 4 + [ANY],
            [shape(len(members) * 4 + 1, *piece)] + [shape(4, *piece, dtype=F32)] * 2,
            "lower",
        )(offsets, got, qt, kt, vt, token)

    def partner(members, column, token, extra=(), turn=()):
        return call(
            functools.partial(partner_kernel, members, extra),
            [SMEM] + [VMEM] * 6 + [ANY] + [VMEM] * len(turn),
            shape(len(members) * 3 + len(extra) * 4 + 1, *piece),
            "partner%d" % members[0],
        )(offsets, kt, vt, q23, *column, token, *turn)

    def mine(members, rows, column, below, token):
        return call(
            functools.partial(mine_kernel, members),
            [SMEM] + [VMEM] * (len(rows) + 7) + [ANY] + [VMEM] * len(below),
            [state] * len(rows),
            "mine%d" % members[0],
            aliases={1 + i: i for i in range(len(rows))},
        )(offsets, *rows, qt, kt, vt, q23, *column, token, *below)

    def finished(members, rows, message, token, extra=()):
        dest = shape(rows_here // 4, len(members) * DH)
        return call(
            functools.partial(finish_kernel, members),
            [SMEM] + [VMEM] * (len(rows) + 1) + [ANY] + [VMEM] * len(extra),
            [dest] * 4 + [state] * len(rows),
            "finish%d" % members[0],
            aliases={1 + i: 4 + i for i in range(len(rows))},
        )(offsets, *rows, message, token, *extra)[:4]

    def project(first, pieces, before, token, final=False):
        model = out_weight.shape[1]
        total = shape(rows_here // 4, model, dtype=BF16 if final else F32)
        scratch = [pltpu.VMEM((rows_here // 4, sum(x.shape[1] for x in pieces)), BF16)]
        if final:
            scratch += [
                pltpu.VMEM((rows_here // 4, model), BF16),
                pltpu.SemaphoreType.DMA((model // 512,)),
            ]
        return call(
            functools.partial(project_kernel, first, len(before), final),
            [VMEM] * (len(pieces) + 1 + len(before)) + [ANY],
            total,
            "project%d" % first,
            scratch=scratch,
            out_spec=ANY if final else VMEM,
        )(*pieces, *before, weights, token)

    def both(members):
        cut = slice(members[0], members[-1] + 1)
        return jnp.stack([kv3[cut], kv3_near[cut]])

    def send(value, axis, pairs):
        return lax.ppermute(value, axis, pairs)

    group_a, group_b, group_c = GROUPS
    *rows_a, = own((0, 1), kv3)
    kv3_near, rows_a[1] = lax.optimization_barrier((kv3_near, rows_a[1]))
    far_a, kv2_a = lax.optimization_barrier((both(group_a), kv2[0]))
    rows_bc = own((2, 3), far_a)
    far_a, kv2_a = send(far_a, "ctx", far), send(kv2_a, "ctx", near)
    msg1, o1, s1 = lower((0, 1), first, rows_bc[0])
    turn = send(msg1, "ctx", swap)
    weights = call(weights_kernel, [VMEM, ANY], shape(*out_weight.shape), "weights")(
        out_weight, msg1
    )

    far_a, kv2_a, far_b, kv2_b, weights = lax.optimization_barrier(
        (far_a, kv2_a, both(group_b), kv2[1], weights)
    )
    far_b_now = far_b
    far_b, kv2_b = send(far_b, "ctx", far), send(kv2_b, "ctx", near)
    column_a = [kv2_a, kv3_near, far_a]
    msg_a = partner(group_a, column_a, far_b_now, (2,), (turn,))
    got_a = send(msg_a, "ctx", swap)
    rows_a = list(mine(group_a, rows_a, column_a, [turn], msg_a))

    far_b, kv2_b, far_c, kv2_c, rows_a[0] = lax.optimization_barrier(
        (far_b, kv2_b, both(group_c), kv2[2], rows_a[0])
    )
    column_b = [kv2_b, kv3_near, far_b]
    msg_b = partner(group_b, column_b, far_c)
    far_c, kv2_c = send(far_c, "ctx", far), send(kv2_c, "ctx", near)
    got_b = send(msg_b, "ctx", swap)
    rows_b = mine(group_b, rows_bc[:2], column_b, [], msg_b)
    rows_a = finished(group_a, rows_a, got_a, rows_b[0])
    a1, a2, a3 = (send(rows_a[t], "head", over[t]) for t in (1, 2, 3))

    column_c = [kv2_c, kv3_near, far_c]
    msg_c = partner(group_c, column_c, rows_a[0])
    got_c = send(msg_c, "ctx", swap)
    rows_b = finished(group_b, rows_b, got_b, msg_c, (got_a,))
    b1, b2, b3 = (send(rows_b[t], "head", over[t]) for t in (1, 2, 3))
    rows_c = mine(group_c, rows_bc[2:], column_c, [o1, s1], rows_b[0])
    half = project(0, [rows_a[0], a1, a2, a3], [], rows_c[0])
    rows_c = finished(group_c, rows_c, got_c, half)
    c1, c2, c3 = (send(rows_c[t], "head", over[t]) for t in (1, 2, 3))
    half = project(8 * DH, [rows_b[0], b1, b2, b3], [half], rows_c[0])
    return project(12 * DH, [rows_c[0], c1, c2, c3], [half], half, final=True)


def solution(mesh):
    placed = (P("ctx", "head"), P("ctx", "head"), P("ctx", "head"), P(), P())
    return jax.shard_map(
        body, mesh=mesh, in_specs=placed, out_specs=P(("ctx", "head"), None), check_vma=False
    )
```

```python
import functools
import math

import jax
import jax.numpy as jnp
from jax import lax
from jax.experimental import pallas as pl
from jax.experimental.pallas import tpu as pltpu
from jax.sharding import PartitionSpec as P

DH = 128
HEADS_HERE = 4
GROUPS = ((0, 1), (2, 3))
PIECES = ((0, 1), (2,), (3,))
RES = 8
SUB = 16
BLK = RES * SUB
NEG = -1e30
RATE = math.log2(math.e) / math.sqrt(DH)
BF16 = jnp.bfloat16
F32 = jnp.float32
VMEM_LIMIT = 20 * 1024 * 1024


COST = {'mine0': 10**10, 'partner2': 10**10, 'lower': 3 * 10**9}


def iota(shape, dim):
    return lax.broadcasted_iota(jnp.int32, shape, dim)


def regroup_matrix(inverse):
    row, col = iota((BLK, BLK), 0), iota((BLK, BLK), 1)
    if inverse:
        hit = col == (row % RES) * SUB + row // RES
    else:
        hit = col == (row % SUB) * RES + row // SUB
    return jnp.where(hit, 1.0, 0.0).astype(BF16)


def causal_bias(position, size):
    rows = position(iota((size, size), 0))
    cols = position(iota((size, size), 1))
    return jnp.where(cols <= rows, 0.0, NEG)


def scores_of(q, blocks):
    scores = []
    for k, _, bias in blocks:
        s = lax.dot_general(q, k, (((1,), (1,)), ((), ())), preferred_element_type=F32)
        scores.append(s if bias is None else s + bias)
    return scores


def finish(scores, blocks):
    wide = scores[0]
    for s in scores[1:]:
        wide = jnp.maximum(wide, s)
    top = jnp.max(wide, axis=1, keepdims=True)
    total = None
    for s, (_, v, _) in zip(scores, blocks):
        p = jnp.exp2((s - top) * RATE).astype(BF16)
        with_ones = jnp.concatenate([v, jnp.ones(v.shape, BF16)], axis=1)
        part = jnp.dot(p, with_ones, preferred_element_type=F32)
        total = part if total is None else total + part
    row_sum = total[:, DH:]
    return total[:, :DH] / row_sum, top * RATE + jnp.log2(row_sum)


def attend_all(tasks):
    held = None
    for load, blocks, put in tasks:
        blocks = blocks()
        scores = scores_of(load(), blocks)
        if held is not None:
            held[2](*finish(held[0], held[1]))
        held = (scores, blocks, put)
    held[2](*finish(held[0], held[1]))


def merge(parts):
    top = parts[0][1]
    for _, lse in parts[1:]:
        top = jnp.maximum(top, lse)
    out, weight = 0.0, 0.0
    for o, lse in parts:
        w = jnp.exp2(lse - top)
        out += o * w
        weight += w
    return out / weight, top + jnp.log2(weight)


def add_rows(out, lse, at, part):
    held = out[at].shape
    was = (out[at].reshape(part[0].shape), lse[at].reshape(part[0].shape))
    o, s = merge([was, part])
    out[at] = o.reshape(held)
    lse[at] = s.reshape(held)


def rows_of(ref, level, shift, first=0, count=None):
    count = ref.shape[0] - first if count is None else count
    return [
        ref[pl.ds(first, count), shift + j * 2**level].reshape(count * SUB, DH)
        for j in range(RES // 2**level)
    ]


def shift_of(off_ref, level, head):
    return off_ref[level - 1, lax.axis_index("head") * HEADS_HERE + head]


def regroup(sources, targets):
    turn = regroup_matrix(False)
    heads, blocks = targets[0].shape[:2]
    for src, dst in zip(sources, targets):
        for b in range(blocks):
            x = src[b * BLK : (b + 1) * BLK, :]
            x = jnp.dot(turn, x, preferred_element_type=F32).astype(BF16)
            for h in range(heads):
                dst[h, b] = x[:, h * DH : (h + 1) * DH].reshape(RES, SUB, DH)


def prep_kv_kernel(off_ref, k_ref, v_ref, kt, vt, kv3, *kv2):
    regroup((k_ref, v_ref), (kt, vt))
    for h in range(kt.shape[0]):
        o2, o3 = (shift_of(off_ref, level, h) for level in (2, 3))
        (g,) = [g for g, members in enumerate(GROUPS) if h in members]
        n = GROUPS[g].index(h)
        for i, src in enumerate((kt, vt)):
            for j, x in enumerate(rows_of(src.at[h], 2, o2)):
                kv2[g][n, i, j] = x
            kv3[h, i] = rows_of(src.at[h], 3, o3)[0]


def prep_q_kernel(off_ref, q_ref, kt, vt, qt, first, q23):
    regroup((q_ref,), (qt,))
    for h in range(qt.shape[0]):
        o2, o3 = (shift_of(off_ref, level, h) for level in (2, 3))
        for j, x in enumerate(rows_of(qt.at[h], 2, o2) + rows_of(qt.at[h], 3, o3)):
            q23[h, j] = x

    @pl.when(lax.axis_index("ctx") % 2 == 1)
    def _():
        for h in range(2):
            for j, x in enumerate(rows_of(qt.at[h], 1, shift_of(off_ref, 1, h))):
                first[4 * h + j] = x

    @pl.when(lax.axis_index("ctx") % 2 == 0)
    def _():
        for i, src in enumerate((kt, vt)):
            for j, x in enumerate(rows_of(src.at[3], 1, shift_of(off_ref, 1, 3))):
                first[4 * i + j] = x


def own_kernel(heads, off_ref, qt, kt, vt, token, *outs):
    blocks = qt.shape[1]
    tasks = []

    def level0(h, n, step):
        head, out, lse = heads[h], outs[2 * h], outs[2 * h + 1]
        size = step * BLK
        bias = causal_bias(lambda r: r // BLK * BLK + r % SUB * RES + r % BLK // SUB, size)
        load = lambda ref, n: ref[head, n * step : (n + 1) * step].reshape(size, DH)

        def put(o, s):
            out[n * step : (n + 1) * step] = o.reshape(step, RES, SUB, DH)
            lse[n * step : (n + 1) * step] = s.reshape(step, RES, SUB, DH)

        tasks.append(
            (
                lambda: load(qt, n),
                lambda: [
                    (load(kt, i), load(vt, i), bias if i == n else None) for i in range(n + 1)
                ],
                put,
            )
        )

    def level1(h, n, step):
        head, out, lse = heads[h], outs[2 * h], outs[2 * h + 1]
        shift = shift_of(off_ref, 1, head)
        rows = step * SUB
        slices = RES // 2
        size = rows * slices
        bias = causal_bias(lambda r: r % rows * slices + r // rows, size)

        def load(ref, n):
            return jnp.concatenate(rows_of(ref.at[head], 1, shift, n * step, step), axis=0)

        def put(o, s):
            for j in range(slices):
                at = (pl.ds(n * step, step), shift + 2 * j)
                fresh = (o[j * rows : (j + 1) * rows], s[j * rows : (j + 1) * rows])
                add_rows(out, lse, at, fresh)

        tasks.append(
            (
                lambda: load(qt, n),
                lambda: [
                    (load(kt, i), load(vt, i), bias if i == n else None) for i in range(n + 1)
                ],
                put,
            )
        )

    for n in range(blocks // 2):
        for h in range(len(heads)):
            level0(h, n, 2)
    for n in range(blocks // 4):
        for h in range(len(heads)):
            level1(h, n, 4)
    attend_all(tasks)


def put_stat(slab, stat, place):
    lane = iota(stat.shape, 1)
    rest = stat
    now = slab[...]
    for i in range(3):
        piece = rest.astype(BF16)
        rest = rest - piece.astype(F32)
        now = jnp.where(lane == place + 32 * i, piece, now)
    slab[...] = now


def get_stat(slab, place):
    lane = iota(slab.shape, 1)
    hit = (lane == place) | (lane == place + 32) | (lane == place + 64)
    return jnp.sum(jnp.where(hit, slab[...].astype(F32), 0.0), axis=1, keepdims=True)


def put_message(msg, place, o, s, count):
    rows = msg.shape[1]
    for j in range(count):
        at = slice(j * rows, (j + 1) * rows)
        msg[place + j] = o[at].astype(BF16)
        put_stat(msg.at[msg.shape[0] - 1], s[at], place + j)


def pair_tasks(load, keys, values, put):
    count = RES // 2

    def blocks():
        k, v = keys(), values()
        return [
            (jnp.concatenate(k[i : i + 2], axis=0), jnp.concatenate(v[i : i + 2], axis=0), None)
            for i in range(0, count, 2)
        ]

    return [
        (
            lambda j=j: jnp.concatenate(load()[j : j + 2], axis=0),
            blocks,
            lambda o, s, j=j: put(j, o, s),
        )
        for j in range(0, count, 2)
    ]


def lower_kernel(heads, off_ref, got, qt, kt, vt, token, msg, *local):
    last = msg.shape[0] - 1
    count = RES // 2
    rows = msg.shape[1]
    later = lax.axis_index("ctx") % 2 == 1
    msg[...] = jnp.zeros(msg.shape, BF16)

    @pl.when(jnp.logical_not(later))
    def _():
        tasks = []
        for n, head in enumerate(heads):
            shift = shift_of(off_ref, 1, head)
            tasks += pair_tasks(
                lambda n=n: [got[n * count + j] for j in range(count)],
                lambda head=head, shift=shift: rows_of(kt.at[head], 1, shift),
                lambda head=head, shift=shift: rows_of(vt.at[head], 1, shift),
                lambda j, o, s, n=n: put_message(msg, n * count + j, o, s, 2),
            )
        attend_all(tasks)
        for ref, fill in zip(local, (0.0, NEG)):
            ref[...] = jnp.full(ref.shape, fill, F32)

    @pl.when(later)
    def _():
        for j, x in enumerate(rows_of(qt.at[2], 1, shift_of(off_ref, 1, 2))):
            msg[j] = x
        shift = shift_of(off_ref, 1, 3)

        def put(j, o, s):
            for i in range(2):
                local[0][j + i] = o[i * rows : (i + 1) * rows]
                local[1][j + i] = s[i * rows : (i + 1) * rows]

        attend_all(
            pair_tasks(
                lambda: rows_of(qt.at[3], 1, shift),
                lambda: [got[j] for j in range(count)],
                lambda: [got[count + j] for j in range(count)],
                put,
            )
        )


def last_kernel(off_ref, turn, kt, vt, token, msg):
    msg[...] = jnp.zeros(msg.shape, BF16)

    @pl.when(lax.axis_index("ctx") % 2 == 0)
    def _():
        shift = shift_of(off_ref, 1, 2)
        attend_all(
            pair_tasks(
                lambda: [turn[j] for j in range(RES // 2)],
                lambda: rows_of(kt.at[2], 1, shift),
                lambda: rows_of(vt.at[2], 1, shift),
                lambda j, o, s: put_message(msg, j, o, s, 2),
            )
        )


def level_blocks(off_ref, level, head, n, q23, kt, vt, kv2, near, far):
    ctx = lax.axis_index("ctx")
    z = ctx // 2
    shift = shift_of(off_ref, level, head)
    count = RES // 2**level
    rows = q23.shape[2]
    size = count * rows
    odd = jnp.where(z % 2 == 1, 0.0, NEG)
    high = jnp.where(z % 4 >= 2, 0.0, NEG)

    def whole(ref):
        return jnp.concatenate(rows_of(ref.at[head], level, shift), axis=0)

    def blocks(bias):
        if level == 2:
            past = [(kv2[n, 0].reshape(size, DH), kv2[n, 1].reshape(size, DH), odd)]
        else:
            past = [
                (near[head, 0], near[head, 1], odd),
                (far[0, n, 0], far[0, n, 1], high),
                (far[1, n, 0], far[1, n, 1], high),
            ]
        return past + [(whole(kt), whole(vt), bias)]

    return whole, blocks, shift, count, rows


def partner_kernel(heads, off_ref, kt, vt, q23, kv2, near, far, token, *msgs):
    later = jnp.where(lax.axis_index("ctx") % 2 == 0, 0.0, NEG)
    tasks = []
    for msg in msgs:
        msg[msg.shape[0] - 1] = jnp.zeros(msg.shape[1:], BF16)
    places = [0] * len(msgs)
    order = [(level, n) for level in (2, 3) for n in range(len(heads))]
    if len(msgs) > 1:
        order.sort(key=lambda item: item[1])
    for level, n in order:
        head, which = heads[n], n % len(msgs)
        _, blocks, _, count, rows = level_blocks(
            off_ref, level, head, n, q23, kt, vt, kv2, near, far
        )
        first = 0 if level == 2 else 2
        tasks.append(
            (
                lambda h=head, f=first, c=count, r=rows: q23[h, f : f + c].reshape(c * r, DH),
                lambda blocks=blocks: blocks(later),
                lambda o, s, m=msgs[which], p=places[which], c=count: put_message(m, p, o, s, c),
            )
        )
        places[which] += count
    attend_all(tasks)


def add_lower(off_ref, head, msg, first, out, lse):
    later = lax.axis_index("ctx") % 2 == 1
    for j in range(RES // 2):
        at = (slice(None), shift_of(off_ref, 1, head) + 2 * j)
        stat = jnp.where(later, get_stat(msg.at[msg.shape[0] - 1], first + j), NEG)
        part = msg[first + j].astype(F32)
        add_rows(out, lse, at, (part, jnp.broadcast_to(stat, part.shape)))


def mine_kernel(heads, which, off_ref, *refs):
    number = len(heads)
    refs = refs[2 * number :]
    (qt, kt, vt, q23, kv2, near, far, token), refs = refs[:8], refs[8:]
    lower, state = refs[: -2 * number], refs[-2 * number :]
    tasks = []
    for level in (2, 3):
        for n, head in enumerate(heads):
            out, lse = state[2 * n : 2 * n + 2]
            whole, blocks, shift, count, rows = level_blocks(
                off_ref, level, head, n, q23, kt, vt, kv2, near, far
            )
            triangle = causal_bias(lambda r, c=count, m=rows: r % m * c + r // m, count * rows)

            def put(o, s, out=out, lse=lse, shift=shift, level=level, count=count, rows=rows):
                for j in range(count):
                    at = slice(j * rows, (j + 1) * rows)
                    add_rows(out, lse, (slice(None), shift + j * 2**level), (o[at], s[at]))

            tasks.append(
                (
                    lambda whole=whole: whole(qt),
                    lambda blocks=blocks, t=triangle: blocks(t)[which],
                    put,
                )
            )
    attend_all(tasks)
    for n, head in enumerate(heads):
        if lower and head == 3:
            for j in range(RES // 2):
                at = (slice(None), shift_of(off_ref, 1, head) + 2 * j)
                add_rows(state[2 * n], state[2 * n + 1], at, (lower[0][j], lower[1][j]))


def finish_kernel(heads, stacked, off_ref, *refs):
    number = len(heads)
    refs = refs[2 * number :]
    msg, token, *below = refs[: -4 - 2 * number]
    dests, state = refs[-4 - 2 * number : -2 * number], refs[-2 * number :]
    for n, head in enumerate(heads):
        if below:
            add_lower(off_ref, head, below[0], n * (RES // 2), state[2 * n], state[2 * n + 1])
    place = 0
    for level in (2, 3):
        for n, head in enumerate(heads):
            shift = shift_of(off_ref, level, head)
            for j in range(RES // 2**level):
                part = msg[place].astype(F32)
                stat = get_stat(msg.at[msg.shape[0] - 1], place)
                add_rows(
                    state[2 * n],
                    state[2 * n + 1],
                    (slice(None), shift + j * 2**level),
                    (part, jnp.broadcast_to(stat, part.shape)),
                )
                place += 1
    mine = lax.axis_index("head")
    per = state[0].shape[0] // 4
    if stacked:
        dests = (dests[0], dests[1], dests[2].at[0], dests[2].at[1])
    for t, dest in enumerate(dests):
        for n in range(number):
            x = state[2 * n][pl.ds((mine ^ t) * per, per)].reshape(per * BLK, DH)
            dest[:, n * DH : (n + 1) * DH] = x.astype(BF16)


def weights_kernel(w_ref, token, out):
    mine = lax.axis_index("head")
    at = 0
    for members in PIECES:
        width = len(members) * DH
        for t in range(4):
            first = (mine ^ t) * (HEADS_HERE * DH) + members[0] * DH
            out[at : at + width, :] = w_ref[pl.ds(pl.multiple_of(first, DH), width), :]
            at += width


def project_kernel(first, added, final, *refs):
    if final:
        *pieces, w_ref, token, out_hbm, plain, out, sems = refs
    else:
        *pieces, w_ref, token, out, plain = refs
    if added:
        *pieces, before = pieces
    back = regroup_matrix(True)
    depth = plain.shape[1]
    for b in range(plain.shape[0] // BLK):
        rows = slice(b * BLK, (b + 1) * BLK)
        x = jnp.concatenate(
            [src[0, rows, :] if len(src.shape) == 3 else src[rows, :] for src in pieces], axis=1
        )
        plain[rows, :] = jnp.dot(back, x, preferred_element_type=F32).astype(BF16)
    tile = 512
    steps = out.shape[1] // tile

    def copy(step):
        cols = pl.ds(pl.multiple_of(step * tile, tile), tile)
        return pltpu.make_async_copy(out.at[:, cols], out_hbm.at[:, cols], sems.at[step])

    @pl.loop(0, steps)
    def _(step):
        cols = pl.ds(pl.multiple_of(step * tile, tile), tile)
        total = jnp.dot(
            plain[...], w_ref[first : first + depth, cols], preferred_element_type=F32
        )
        if added:
            total = total + before[:, cols]
        out[:, cols] = total.astype(out.dtype)
        if final:
            copy(step).start()

    if final:

        @pl.loop(0, steps)
        def _(step):
            copy(step).wait()


SMEM = pl.BlockSpec(memory_space=pltpu.SMEM)
VMEM = pl.BlockSpec(memory_space=pltpu.VMEM)
ANY = pl.BlockSpec(memory_space=pl.ANY)


def shape(*dims, dtype=BF16):
    return jax.ShapeDtypeStruct(dims, dtype)


def call(kernel, specs, outs, name, scratch=(), aliases={}, out_spec=VMEM):
    return pl.pallas_call(
        kernel,
        in_specs=specs,
        out_specs=jax.tree.map(lambda _: out_spec, outs),
        out_shape=outs,
        scratch_shapes=scratch,
        input_output_aliases=aliases,
        compiler_params=pltpu.CompilerParams(vmem_limit_bytes=VMEM_LIMIT),
        cost_estimate=pl.CostEstimate(flops=COST.get(name, 10**9), bytes_accessed=1, transcendentals=0),
        name=name,
    )


def body(queries, keys, values, offsets, out_weight):
    rows_here, width = queries.shape
    blocks = rows_here // BLK
    heads = width // DH
    slots = rows_here // RES
    piece = (slots, DH)
    regrouped = shape(heads, blocks, RES, SUB, DH)
    ctx_size = lax.axis_size("ctx")
    swap = [(i, i ^ 1) for i in range(ctx_size)]
    near = [(i, i ^ 2) for i in range(ctx_size)]
    far = [(i, i ^ 4) for i in range(ctx_size)]
    over = [[(i, i ^ t) for i in range(4)] for t in range(4)]

    kt, vt, kv3, *kv2 = call(
        prep_kv_kernel,
        [SMEM, VMEM, VMEM],
        [regrouped, regrouped, shape(heads, 2, *piece)]
        + [shape(len(members), 2, 2, *piece) for members in GROUPS],
        "prep_kv",
    )(offsets, keys, values)
    kv3_near = lax.ppermute(kv3, "ctx", near)
    qt, first, q23 = call(
        prep_q_kernel,
        [SMEM, VMEM, VMEM, VMEM],
        [regrouped, shape(8, *piece), shape(heads, 3, *piece)],
        "prep_q",
    )(offsets, queries, kt, vt)
    first = lax.ppermute(first, "ctx", swap)

    state = shape(blocks, RES, SUB, DH, dtype=F32)

    def own(members, token):
        return call(
            functools.partial(own_kernel, members),
            [SMEM, VMEM, VMEM, VMEM, ANY],
            [state] * (2 * len(members)),
            "own%d" % members[0],
        )(offsets, qt, kt, vt, token)

    def lower(members, got, token):
        return call(
            functools.partial(lower_kernel, members),
            [SMEM] + [VMEM] * 4 + [ANY],
            [shape(len(members) * 4 + 1, *piece)] + [shape(4, *piece, dtype=F32)] * 2,
            "lower",
        )(offsets, got, qt, kt, vt, token)

    def partner(members, column, token, messages):
        return call(
            functools.partial(partner_kernel, members),
            [SMEM] + [VMEM] * 6 + [ANY],
            [shape(len(members) // messages * 3 + 1, *piece)] * messages,
            "partner%d" % members[0],
        )(offsets, kt, vt, q23, *column, token)

    def mine(members, rows, column, below, token, which=slice(None), name="mine"):
        return call(
            functools.partial(mine_kernel, members, which),
            [SMEM] + [VMEM] * (len(rows) + 7) + [ANY] + [VMEM] * len(below),
            [state] * len(rows),
            name + "%d" % members[0],
            aliases={1 + i: i for i in range(len(rows))},
        )(offsets, *rows, qt, kt, vt, q23, *column, token, *below)

    def finished(members, rows, message, token, *below):
        dest = shape(rows_here // 4, len(members) * DH)
        stacked = members != PIECES[-1]
        dests = [dest, dest, shape(2, *dest.shape), shape(8, DH)] if stacked else [dest] * 4
        return call(
            functools.partial(finish_kernel, members, stacked),
            [SMEM] + [VMEM] * (len(rows) + 1) + [ANY] + [VMEM] * len(below),
            dests + [state] * len(rows),
            "finish%d" % members[0],
            aliases={1 + i: 4 + i for i in range(len(rows))},
        )(offsets, *rows, message, token, *below)[:4]

    def project(first, pieces, before, token, final=False):
        model = out_weight.shape[1]
        total = shape(rows_here // 4, model, dtype=BF16 if final else F32)
        scratch = [pltpu.VMEM((rows_here // 4, sum(x.shape[-1] for x in pieces)), BF16)]
        if final:
            scratch += [
                pltpu.VMEM((rows_here // 4, model), BF16),
                pltpu.SemaphoreType.DMA((model // 512,)),
            ]
        return call(
            functools.partial(project_kernel, first, len(before), final),
            [VMEM] * (len(pieces) + 1 + len(before)) + [ANY],
            total,
            "project%d" % first,
            scratch=scratch,
            out_spec=ANY if final else VMEM,
        )(*pieces, *before, weights, token)

    def both(members):
        cut = slice(members[0], members[-1] + 1)
        return jnp.stack([kv3[cut], kv3_near[cut]])

    def send(value, axis, pairs):
        return lax.ppermute(value, axis, pairs)

    group_a, group_b = GROUPS
    *rows_a, = own((0, 1), kv3)
    kv3_near, rows_a[1] = lax.optimization_barrier((kv3_near, rows_a[1]))
    far_a, kv2_a, q23 = lax.optimization_barrier((both(group_a), kv2[0], q23))
    rows_b = own((2, 3), far_a)
    far_a, kv2_a = send(far_a, "ctx", far), send(kv2_a, "ctx", near)
    q23 = send(q23, "ctx", swap)
    msg1, o1, s1 = lower((0, 1), first, rows_b[0])
    turn = send(msg1, "ctx", swap)
    weights = call(weights_kernel, [VMEM, ANY], shape(*out_weight.shape), "weights")(
        out_weight, msg1
    )

    far_a, kv2_a, far_b, kv2_b, weights = lax.optimization_barrier(
        (far_a, kv2_a, both(group_b), kv2[1], weights)
    )
    ready = far_b
    far_b, kv2_b = send(far_b, "ctx", far), send(kv2_b, "ctx", near)
    column_a = [kv2_a, kv3_near, far_a]
    (msg_a,) = partner(group_a, column_a, ready, 1)
    got_a = send(msg_a, "ctx", swap)
    rows_a = list(mine(group_a, rows_a, column_a, [], msg_a))
    msg1c = call(
        last_kernel, [SMEM] + [VMEM] * 3 + [ANY], shape(RES // 2 + 1, *piece), "last"
    )(offsets, turn, kt, vt, rows_a[0])
    got1c = send(msg1c, "ctx", swap)
    rows_a = finished(group_a, rows_a, got_a, msg1c, turn)
    a1, a23 = send(rows_a[1], "head", over[1]), send(rows_a[2], "head", over[2])

    column_b = [kv2_b, kv3_near, far_b]
    msg_b, msg_c = partner(group_b, column_b, rows_a[0], 2)
    got_b, got_c = send(msg_b, "ctx", swap), send(msg_c, "ctx", swap)
    rows_b = mine(group_b, rows_b, column_b, [o1, s1], msg_c)
    a23, *rows_b = lax.optimization_barrier((a23, *rows_b))
    a3 = send(a23[1], "head", over[1])
    rows_b, rows_c = rows_b[:2], rows_b[2:]
    rows_b = finished((2,), rows_b, got_b, rows_c[0], got1c)
    b1, b23 = send(rows_b[1], "head", over[1]), send(rows_b[2], "head", over[2])
    rows_c = finished((3,), rows_c, got_c, rows_b[0])
    c2, c3, c1 = (send(rows_c[t], "head", over[t]) for t in (2, 3, 1))
    half = project(0, [rows_a[0], a1, a23, a3], [], rows_c[0])
    b23, half = lax.optimization_barrier((b23, half))
    b3 = send(b23[1], "head", over[1])
    half = project(8 * DH, [rows_b[0], b1, b23, b3, rows_c[0], c1], [half], half)
    return project(14 * DH, [c2, c3], [half], half, final=True)


def solution(mesh):
    placed = (P("ctx", "head"), P("ctx", "head"), P("ctx", "head"), P(), P())
    return jax.shard_map(
        body, mesh=mesh, in_specs=placed, out_specs=P(("ctx", "head"), None), check_vma=False
    )
```

```python
import functools
import math

import jax
import jax.numpy as jnp
from jax import lax
from jax.experimental import pallas as pl
from jax.experimental.pallas import tpu as pltpu
from jax.sharding import PartitionSpec as P

DH = 128
HEADS_HERE = 4
GROUPS = ((0, 1), (2, 3))
PIECES = ((0, 1), (2,), (3,))
RES = 8
SUB = 16
BLK = RES * SUB
TAIL = 64
NEG = -1e30
RATE = math.log2(math.e) / math.sqrt(DH)
BF16 = jnp.bfloat16
F32 = jnp.float32
VMEM_LIMIT = 20 * 1024 * 1024


COST = {'mine0': 10**10, 'partner2': 10**10, 'lower': 3 * 10**9}


def iota(shape, dim):
    return lax.broadcasted_iota(jnp.int32, shape, dim)


def regroup_matrix(inverse):
    row, col = iota((BLK, BLK), 0), iota((BLK, BLK), 1)
    if inverse:
        hit = col == (row % RES) * SUB + row // RES
    else:
        hit = col == (row % SUB) * RES + row // SUB
    return jnp.where(hit, 1.0, 0.0).astype(BF16)


def causal_bias(position, size):
    rows = position(iota((size, size), 0))
    cols = position(iota((size, size), 1))
    return jnp.where(cols <= rows, 0.0, NEG)


def scores_of(q, blocks):
    scores = []
    for k, _, bias in blocks:
        s = lax.dot_general(q, k, (((1,), (1,)), ((), ())), preferred_element_type=F32)
        scores.append(s if bias is None else s + bias)
    return scores


def finish(scores, blocks):
    wide = scores[0]
    for s in scores[1:]:
        wide = jnp.maximum(wide, s)
    top = jnp.max(wide, axis=1, keepdims=True)
    total = None
    for s, (_, v, _) in zip(scores, blocks):
        p = jnp.exp2((s - top) * RATE).astype(BF16)
        with_ones = jnp.concatenate([v, jnp.ones(v.shape, BF16)], axis=1)
        part = jnp.dot(p, with_ones, preferred_element_type=F32)
        total = part if total is None else total + part
    row_sum = total[:, DH:]
    return total[:, :DH] / row_sum, top * RATE + jnp.log2(row_sum)


def attend_all(tasks):
    held = None
    for load, blocks, put in tasks:
        blocks = blocks()
        scores = scores_of(load(), blocks)
        if held is not None:
            held[2](*finish(held[0], held[1]))
        held = (scores, blocks, put)
    held[2](*finish(held[0], held[1]))


def merge(parts):
    top = parts[0][1]
    for _, lse in parts[1:]:
        top = jnp.maximum(top, lse)
    out, weight = 0.0, 0.0
    for o, lse in parts:
        w = jnp.exp2(lse - top)
        out += o * w
        weight += w
    return out / weight, top + jnp.log2(weight)


def add_rows(out, lse, at, part):
    held = out[at].shape
    was = (out[at].reshape(part[0].shape), lse[at].reshape(part[0].shape))
    o, s = merge([was, part])
    out[at] = o.reshape(held)
    lse[at] = s.reshape(held)


def rows_of(ref, level, shift, first=0, count=None):
    count = ref.shape[0] - first if count is None else count
    return [
        ref[pl.ds(first, count), shift + j * 2**level].reshape(count * SUB, DH)
        for j in range(RES // 2**level)
    ]


def shift_of(off_ref, level, head):
    return off_ref[level - 1, lax.axis_index("head") * HEADS_HERE + head]


def regroup(sources, targets):
    turn = regroup_matrix(False)
    heads, blocks = targets[0].shape[:2]
    for src, dst in zip(sources, targets):
        for b in range(blocks):
            x = src[b * BLK : (b + 1) * BLK, :]
            x = jnp.dot(turn, x, preferred_element_type=F32).astype(BF16)
            for h in range(heads):
                dst[h, b] = x[:, h * DH : (h + 1) * DH].reshape(RES, SUB, DH)


def prep_kv_kernel(off_ref, k_ref, v_ref, kt, vt, kv3, *kv2):
    regroup((k_ref, v_ref), (kt, vt))
    for h in range(kt.shape[0]):
        o2, o3 = (shift_of(off_ref, level, h) for level in (2, 3))
        (g,) = [g for g, members in enumerate(GROUPS) if h in members]
        n = GROUPS[g].index(h)
        for i, src in enumerate((kt, vt)):
            for j, x in enumerate(rows_of(src.at[h], 2, o2)):
                kv2[g][n, i, j] = x
            kv3[h, i] = rows_of(src.at[h], 3, o3)[0]


def prep_q_kernel(off_ref, q_ref, kt, vt, qt, first, q23):
    regroup((q_ref,), (qt,))
    for h in range(qt.shape[0]):
        o2, o3 = (shift_of(off_ref, level, h) for level in (2, 3))
        for j, x in enumerate(rows_of(qt.at[h], 2, o2) + rows_of(qt.at[h], 3, o3)):
            q23[h, j] = x

    @pl.when(lax.axis_index("ctx") % 2 == 1)
    def _():
        for h in range(2):
            for j, x in enumerate(rows_of(qt.at[h], 1, shift_of(off_ref, 1, h))):
                first[4 * h + j] = x

    @pl.when(lax.axis_index("ctx") % 2 == 0)
    def _():
        for i, src in enumerate((kt, vt)):
            for j, x in enumerate(rows_of(src.at[3], 1, shift_of(off_ref, 1, 3))):
                first[4 * i + j] = x


def own_kernel(heads, off_ref, qt, kt, vt, token, *outs):
    blocks = qt.shape[1]
    tasks = []

    def level0(h, n, step):
        head, out, lse = heads[h], outs[2 * h], outs[2 * h + 1]
        size = step * BLK
        bias = causal_bias(lambda r: r // BLK * BLK + r % SUB * RES + r % BLK // SUB, size)
        load = lambda ref, n: ref[head, n * step : (n + 1) * step].reshape(size, DH)

        def put(o, s):
            out[n * step : (n + 1) * step] = o.reshape(step, RES, SUB, DH)
            lse[n * step : (n + 1) * step] = s.reshape(step, RES, SUB, DH)

        tasks.append(
            (
                lambda: load(qt, n),
                lambda: [
                    (load(kt, i), load(vt, i), bias if i == n else None) for i in range(n + 1)
                ],
                put,
            )
        )

    def level1(h, n, step):
        head, out, lse = heads[h], outs[2 * h], outs[2 * h + 1]
        shift = shift_of(off_ref, 1, head)
        rows = step * SUB
        slices = RES // 2
        size = rows * slices
        bias = causal_bias(lambda r: r % rows * slices + r // rows, size)

        def load(ref, n):
            return jnp.concatenate(rows_of(ref.at[head], 1, shift, n * step, step), axis=0)

        def put(o, s):
            for j in range(slices):
                at = (pl.ds(n * step, step), shift + 2 * j)
                fresh = (o[j * rows : (j + 1) * rows], s[j * rows : (j + 1) * rows])
                add_rows(out, lse, at, fresh)

        tasks.append(
            (
                lambda: load(qt, n),
                lambda: [
                    (load(kt, i), load(vt, i), bias if i == n else None) for i in range(n + 1)
                ],
                put,
            )
        )

    for n in range(blocks // 2):
        for h in range(len(heads)):
            level0(h, n, 2)
    for n in range(blocks // 4):
        for h in range(len(heads)):
            level1(h, n, 4)
    attend_all(tasks)


def put_message(msg, slab, place, o, s, count):
    rows = o.shape[0] // count
    lane = iota((rows, DH), 1)
    for j in range(count):
        at = slice(j * rows, (j + 1) * rows)
        msg[(place + j) * rows : (place + j + 1) * rows, :] = o[at].astype(BF16)
        rest, now = s[at], slab[:rows, :]
        for i in range(3):
            piece = rest.astype(BF16)
            rest = rest - piece.astype(F32)
            now = jnp.where(lane == 3 * (place + j) + i, piece, now)
        slab[:rows, :] = now


def unit(rows):
    hit = iota((rows, DH), 0) == iota((rows, DH), 1)
    return jnp.where(hit, 1.0, 0.0).astype(BF16)


def close_message(msg, slab):
    first = msg.shape[0] - TAIL
    half = TAIL // 2
    turned = lax.dot_general(
        unit(half), slab[...], (((1,), (1,)), ((), ())), preferred_element_type=F32
    ).astype(BF16)
    for i in range(2):
        msg[first + i * half : first + (i + 1) * half, :] = turned[:, i * DH : (i + 1) * DH]


def open_message(msg, rows):
    first = msg.shape[0] - TAIL
    half = TAIL // 2
    parts = [
        lax.dot_general(
            msg[first + i * half : first + (i + 1) * half, :],
            unit(half),
            (((0,), (0,)), ((), ())),
            preferred_element_type=F32,
        )
        for i in range(2)
    ]
    return jnp.concatenate(parts, axis=0)[:rows]


def get_stat(slab, place):
    lane = iota(slab.shape, 1)
    hit = (lane >= 3 * place) & (lane < 3 * place + 3)
    return jnp.sum(jnp.where(hit, slab, 0.0), axis=1, keepdims=True)


def pair_tasks(load, keys, values, put):
    count = RES // 2

    def blocks():
        k, v = keys(), values()
        return [
            (jnp.concatenate(k[i : i + 2], axis=0), jnp.concatenate(v[i : i + 2], axis=0), None)
            for i in range(0, count, 2)
        ]

    return [
        (
            lambda j=j: jnp.concatenate(load()[j : j + 2], axis=0),
            blocks,
            lambda o, s, j=j: put(j, o, s),
        )
        for j in range(0, count, 2)
    ]


def lower_kernel(heads, off_ref, got, qt, kt, vt, token, msg, *refs):
    *local, slab = refs
    count = RES // 2
    rows = kt.shape[1] * SUB
    later = lax.axis_index("ctx") % 2 == 1
    msg[...] = jnp.zeros(msg.shape, BF16)
    slab[...] = jnp.zeros(slab.shape, BF16)

    @pl.when(jnp.logical_not(later))
    def _():
        tasks = []
        for n, head in enumerate(heads):
            shift = shift_of(off_ref, 1, head)
            tasks += pair_tasks(
                lambda n=n: [got[n * count + j] for j in range(count)],
                lambda head=head, shift=shift: rows_of(kt.at[head], 1, shift),
                lambda head=head, shift=shift: rows_of(vt.at[head], 1, shift),
                lambda j, o, s, n=n: put_message(msg, slab, n * count + j, o, s, 2),
            )
        attend_all(tasks)
        close_message(msg, slab)
        for ref, fill in zip(local, (0.0, NEG)):
            ref[...] = jnp.full(ref.shape, fill, F32)

    @pl.when(later)
    def _():
        for j, x in enumerate(rows_of(qt.at[2], 1, shift_of(off_ref, 1, 2))):
            msg[j * rows : (j + 1) * rows, :] = x
        shift = shift_of(off_ref, 1, 3)

        def put(j, o, s):
            for i in range(2):
                local[0][j + i] = o[i * rows : (i + 1) * rows]
                local[1][j + i] = s[i * rows : (i + 1) * rows]

        attend_all(
            pair_tasks(
                lambda: rows_of(qt.at[3], 1, shift),
                lambda: [got[j] for j in range(count)],
                lambda: [got[count + j] for j in range(count)],
                put,
            )
        )


def last_kernel(off_ref, turn, kt, vt, token, msg, slab):
    msg[...] = jnp.zeros(msg.shape, BF16)
    slab[...] = jnp.zeros(slab.shape, BF16)
    rows = kt.shape[1] * SUB

    @pl.when(lax.axis_index("ctx") % 2 == 0)
    def _():
        shift = shift_of(off_ref, 1, 2)
        attend_all(
            pair_tasks(
                lambda: [turn[j * rows : (j + 1) * rows, :] for j in range(RES // 2)],
                lambda: rows_of(kt.at[2], 1, shift),
                lambda: rows_of(vt.at[2], 1, shift),
                lambda j, o, s: put_message(msg, slab, j, o, s, 2),
            )
        )
        close_message(msg, slab)


def level_blocks(off_ref, level, head, n, kt, vt, kv2, near, far):
    ctx = lax.axis_index("ctx")
    z = ctx // 2
    shift = shift_of(off_ref, level, head)
    count = RES // 2**level
    rows = kt.shape[1] * SUB
    size = count * rows
    odd = jnp.where(z % 2 == 1, 0.0, NEG)
    high = jnp.where(z % 4 >= 2, 0.0, NEG)

    def whole(ref):
        return jnp.concatenate(rows_of(ref.at[head], level, shift), axis=0)

    def blocks(bias, which="all"):
        past = []
        if which != "own" and level == 2:
            past = [(kv2[n, 0].reshape(size, DH), kv2[n, 1].reshape(size, DH), odd)]
        elif which != "own":
            past = [
                (near[head, 0], near[head, 1], odd),
                (far[0, n, 0], far[0, n, 1], high),
                (far[1, n, 0], far[1, n, 1], high),
            ]
        return past if which == "past" else past + [(whole(kt), whole(vt), bias)]

    return whole, blocks, shift, count, rows


def partner_kernel(heads, off_ref, kt, vt, q23, kv2, near, far, token, *refs):
    later = jnp.where(lax.axis_index("ctx") % 2 == 0, 0.0, NEG)
    tasks = []
    msgs, slabs = refs[: len(refs) // 2], refs[len(refs) // 2 :]
    for slab in slabs:
        slab[...] = jnp.zeros(slab.shape, BF16)
    places = [0] * len(msgs)
    order = [(level, n) for level in (2, 3) for n in range(len(heads))]
    if len(msgs) > 1:
        order.sort(key=lambda item: item[1])
    for level, n in order:
        head, which = heads[n], n % len(msgs)
        _, blocks, _, count, rows = level_blocks(
            off_ref, level, head, n, kt, vt, kv2, near, far
        )
        first = 0 if level == 2 else 2
        tasks.append(
            (
                lambda h=head, f=first, c=count, r=rows: q23[h, f : f + c].reshape(c * r, DH),
                lambda blocks=blocks: blocks(later),
                lambda o, s, w=which, p=places[which], c=count: put_message(
                    msgs[w], slabs[w], p, o, s, c
                ),
            )
        )
        places[which] += count
    attend_all(tasks)
    for msg, slab in zip(msgs, slabs):
        close_message(msg, slab)


def add_message(msg, slab, place, out, lse, at, valid=None):
    rows = slab.shape[0]
    stat = get_stat(slab, place)
    if valid is not None:
        stat = jnp.where(valid, stat, NEG)
    part = msg[place * rows : (place + 1) * rows, :].astype(F32)
    add_rows(out, lse, at, (part, jnp.broadcast_to(stat, part.shape)))


def own_rows(heads, which, off_ref, qt, kt, vt, kv2, near, far, state):
    tasks = []
    for level in (2, 3):
        for n, head in enumerate(heads):
            out, lse = state[2 * n : 2 * n + 2]
            whole, blocks, shift, count, rows = level_blocks(
                off_ref, level, head, n, kt, vt, kv2, near, far
            )
            triangle = causal_bias(lambda r, c=count, m=rows: r % m * c + r // m, count * rows)

            def put(o, s, out=out, lse=lse, shift=shift, level=level, count=count, rows=rows):
                for j in range(count):
                    at = slice(j * rows, (j + 1) * rows)
                    add_rows(out, lse, (slice(None), shift + j * 2**level), (o[at], s[at]))

            tasks.append(
                (
                    lambda whole=whole: whole(qt),
                    lambda blocks=blocks, t=triangle: blocks(t, which),
                    put,
                )
            )
    attend_all(tasks)


def mine_kernel(heads, which, off_ref, *refs):
    number = len(heads)
    refs = refs[2 * number :]
    own_rows(heads, which, off_ref, *refs[:6], refs[7:])


def weights_kernel(off_ref, *refs):
    heads = GROUPS[1]
    number = len(heads)
    qt, kt, vt, o1, s1, w_ref, token, *refs = refs[2 * number :]
    state, out = refs[:-1], refs[-1]
    mine = lax.axis_index("head")
    at = 0
    for members in PIECES:
        width = len(members) * DH
        for t in range(4):
            first = (mine ^ t) * (HEADS_HERE * DH) + members[0] * DH
            out[at : at + width, :] = w_ref[pl.ds(pl.multiple_of(first, DH), width), :]
            at += width
    own_rows(heads, "own", off_ref, qt, kt, vt, None, None, None, state)
    for j in range(RES // 2):
        at = (slice(None), shift_of(off_ref, 1, 3) + 2 * j)
        add_rows(state[-2], state[-1], at, (o1[j], s1[j]))


def finish_kernel(heads, stacked, off_ref, *refs):
    number = len(heads)
    refs = refs[2 * number :]
    msg, token, *below = refs[: -4 - 2 * number]
    dests, state = refs[-4 - 2 * number : -2 * number], refs[-2 * number :]
    rows = state[0].shape[0] * SUB
    later = lax.axis_index("ctx") % 2 == 1
    if below:
        slab = open_message(below[0], rows)
        for n, head in enumerate(heads):
            for j in range(RES // 2):
                at = (slice(None), shift_of(off_ref, 1, head) + 2 * j)
                place = n * (RES // 2) + j
                add_message(below[0], slab, place, state[2 * n], state[2 * n + 1], at, later)
    slab = open_message(msg, rows)
    place = 0
    for level in (2, 3):
        for n, head in enumerate(heads):
            shift = shift_of(off_ref, level, head)
            for j in range(RES // 2**level):
                at = (slice(None), shift + j * 2**level)
                add_message(msg, slab, place, state[2 * n], state[2 * n + 1], at)
                place += 1
    mine = lax.axis_index("head")
    per = state[0].shape[0] // 4
    if stacked:
        dests = (dests[0], dests[1], dests[2].at[0], dests[2].at[1])
    for t, dest in enumerate(dests):
        for n in range(number):
            x = state[2 * n][pl.ds((mine ^ t) * per, per)].reshape(per * BLK, DH)
            dest[:, n * DH : (n + 1) * DH] = x.astype(BF16)


def project_kernel(first, added, final, *refs):
    if final:
        *pieces, w_ref, token, out_hbm, plain, out, sems = refs
    else:
        *pieces, w_ref, token, out, plain = refs
    if added:
        *pieces, before = pieces
    back = regroup_matrix(True)
    depth = plain.shape[1]
    for b in range(plain.shape[0] // BLK):
        rows = slice(b * BLK, (b + 1) * BLK)
        x = jnp.concatenate(
            [src[0, rows, :] if len(src.shape) == 3 else src[rows, :] for src in pieces], axis=1
        )
        plain[rows, :] = jnp.dot(back, x, preferred_element_type=F32).astype(BF16)
    tile = 512
    steps = out.shape[1] // tile

    def copy(step):
        cols = pl.ds(pl.multiple_of(step * tile, tile), tile)
        return pltpu.make_async_copy(out.at[:, cols], out_hbm.at[:, cols], sems.at[step])

    @pl.loop(0, steps)
    def _(step):
        cols = pl.ds(pl.multiple_of(step * tile, tile), tile)
        total = jnp.dot(
            plain[...], w_ref[first : first + depth, cols], preferred_element_type=F32
        )
        if added:
            total = total + before[:, cols]
        out[:, cols] = total.astype(out.dtype)
        if final:
            copy(step).start()

    if final:

        @pl.loop(0, steps)
        def _(step):
            copy(step).wait()


SMEM = pl.BlockSpec(memory_space=pltpu.SMEM)
VMEM = pl.BlockSpec(memory_space=pltpu.VMEM)
ANY = pl.BlockSpec(memory_space=pl.ANY)


def shape(*dims, dtype=BF16):
    return jax.ShapeDtypeStruct(dims, dtype)


def call(kernel, specs, outs, name, scratch=(), aliases={}, out_spec=VMEM):
    return pl.pallas_call(
        kernel,
        in_specs=specs,
        out_specs=jax.tree.map(lambda _: out_spec, outs),
        out_shape=outs,
        scratch_shapes=scratch,
        input_output_aliases=aliases,
        compiler_params=pltpu.CompilerParams(vmem_limit_bytes=VMEM_LIMIT),
        cost_estimate=pl.CostEstimate(flops=COST.get(name, 10**9), bytes_accessed=1, transcendentals=0),
        name=name,
    )


def body(queries, keys, values, offsets, out_weight):
    rows_here, width = queries.shape
    blocks = rows_here // BLK
    heads = width // DH
    slots = rows_here // RES
    piece = (slots, DH)
    message = lambda count: shape(count * slots + TAIL, DH)
    slab = pltpu.VMEM((2 * DH, DH), BF16)
    regrouped = shape(heads, blocks, RES, SUB, DH)
    ctx_size = lax.axis_size("ctx")
    swap = [(i, i ^ 1) for i in range(ctx_size)]
    near = [(i, i ^ 2) for i in range(ctx_size)]
    far = [(i, i ^ 4) for i in range(ctx_size)]
    over = [[(i, i ^ t) for i in range(4)] for t in range(4)]

    kt, vt, kv3, *kv2 = call(
        prep_kv_kernel,
        [SMEM, VMEM, VMEM],
        [regrouped, regrouped, shape(heads, 2, *piece)]
        + [shape(len(members), 2, 2, *piece) for members in GROUPS],
        "prep_kv",
    )(offsets, keys, values)
    kv3_near = lax.ppermute(kv3, "ctx", near)
    qt, first, q23 = call(
        prep_q_kernel,
        [SMEM, VMEM, VMEM, VMEM],
        [regrouped, shape(8, *piece), shape(heads, 3, *piece)],
        "prep_q",
    )(offsets, queries, kt, vt)
    first = lax.ppermute(first, "ctx", swap)

    state = shape(blocks, RES, SUB, DH, dtype=F32)

    def own(members, token):
        return call(
            functools.partial(own_kernel, members),
            [SMEM, VMEM, VMEM, VMEM, ANY],
            [state] * (2 * len(members)),
            "own%d" % members[0],
        )(offsets, qt, kt, vt, token)

    def lower(members, got, token):
        return call(
            functools.partial(lower_kernel, members),
            [SMEM] + [VMEM] * 4 + [ANY],
            [message(len(members) * 4)] + [shape(4, *piece, dtype=F32)] * 2,
            "lower",
            scratch=[slab],
        )(offsets, got, qt, kt, vt, token)

    def partner(members, column, token, messages):
        return call(
            functools.partial(partner_kernel, members),
            [SMEM] + [VMEM] * 6 + [ANY],
            [message(len(members) // messages * 3)] * messages,
            "partner%d" % members[0],
            scratch=[slab] * messages,
        )(offsets, kt, vt, q23, *column, token)

    def mine(members, rows, column, token, which="all"):
        return call(
            functools.partial(mine_kernel, members, which),
            [SMEM] + [VMEM] * (len(rows) + 6) + [ANY],
            [state] * len(rows),
            "mine%d" % members[0],
            aliases={1 + i: i for i in range(len(rows))},
        )(offsets, *rows, qt, kt, vt, *column, token)

    def finished(members, rows, message, token, *below):
        dest = shape(rows_here // 4, len(members) * DH)
        stacked = members != PIECES[-1]
        dests = [dest, dest, shape(2, *dest.shape), shape(8, DH)] if stacked else [dest] * 4
        return call(
            functools.partial(finish_kernel, members, stacked),
            [SMEM] + [VMEM] * (len(rows) + 1) + [ANY] + [VMEM] * len(below),
            dests + [state] * len(rows),
            "finish%d" % members[0],
            aliases={1 + i: 4 + i for i in range(len(rows))},
        )(offsets, *rows, message, token, *below)[:4]

    def project(first, pieces, before, token, final=False):
        model = out_weight.shape[1]
        total = shape(rows_here // 4, model, dtype=BF16 if final else F32)
        scratch = [pltpu.VMEM((rows_here // 4, sum(x.shape[-1] for x in pieces)), BF16)]
        if final:
            scratch += [
                pltpu.VMEM((rows_here // 4, model), BF16),
                pltpu.SemaphoreType.DMA((model // 512,)),
            ]
        return call(
            functools.partial(project_kernel, first, len(before), final),
            [VMEM] * (len(pieces) + 1 + len(before)) + [ANY],
            total,
            "project%d" % first,
            scratch=scratch,
            out_spec=ANY if final else VMEM,
        )(*pieces, *before, weights, token)

    def both(members):
        cut = slice(members[0], members[-1] + 1)
        return jnp.stack([kv3[cut], kv3_near[cut]])

    def send(value, axis, pairs):
        return lax.ppermute(value, axis, pairs)

    group_a, group_b = GROUPS
    *rows_a, = own((0, 1), kv3)
    kv3_near, rows_a[1] = lax.optimization_barrier((kv3_near, rows_a[1]))
    far_a, kv2_a, q23 = lax.optimization_barrier((both(group_a), kv2[0], q23))
    rows_b = own((2, 3), far_a)
    far_a, kv2_a = send(far_a, "ctx", far), send(kv2_a, "ctx", near)
    q23 = send(q23, "ctx", swap)
    msg1, o1, s1 = lower((0, 1), first, rows_b[0])
    turn = send(msg1, "ctx", swap)
    *rows_b, weights = call(
        weights_kernel,
        [SMEM] + [VMEM] * 10 + [ANY],
        [state] * 4 + [shape(*out_weight.shape)],
        "weights",
        aliases={1 + i: i for i in range(4)},
    )(offsets, *rows_b, qt, kt, vt, o1, s1, out_weight, msg1)

    far_a, kv2_a, far_b, kv2_b, weights = lax.optimization_barrier(
        (far_a, kv2_a, both(group_b), kv2[1], weights)
    )
    ready = far_b
    far_b, kv2_b = send(far_b, "ctx", far), send(kv2_b, "ctx", near)
    column_a = [kv2_a, kv3_near, far_a]
    (msg_a,) = partner(group_a, column_a, ready, 1)
    got_a = send(msg_a, "ctx", swap)
    rows_a = list(mine(group_a, rows_a, column_a, msg_a))
    msg1c = call(
        last_kernel,
        [SMEM] + [VMEM] * 3 + [ANY],
        message(RES // 2),
        "last",
        scratch=[slab],
    )(offsets, turn, kt, vt, rows_a[0])
    got1c = send(msg1c, "ctx", swap)
    rows_a = finished(group_a, rows_a, got_a, msg1c, turn)
    a1, a23 = send(rows_a[1], "head", over[1]), send(rows_a[2], "head", over[2])

    column_b = [kv2_b, kv3_near, far_b]
    msg_b, msg_c = partner(group_b, column_b, rows_a[0], 2)
    got_b, got_c = send(msg_b, "ctx", swap), send(msg_c, "ctx", swap)
    rows_b = mine(group_b, rows_b, column_b, msg_c, "past")
    a23, *rows_b = lax.optimization_barrier((a23, *rows_b))
    a3 = send(a23[1], "head", over[1])
    rows_b, rows_c = rows_b[:2], rows_b[2:]
    rows_b = finished((2,), rows_b, got_b, rows_c[0], got1c)
    b1, b23 = send(rows_b[1], "head", over[1]), send(rows_b[2], "head", over[2])
    rows_c = finished((3,), rows_c, got_c, rows_b[0])
    c2, c3, c1 = (send(rows_c[t], "head", over[t]) for t in (2, 3, 1))
    half = project(0, [rows_a[0], a1, a23, a3, rows_b[0], b1], [], rows_c[0])
    b23, half = lax.optimization_barrier((b23, half))
    b3 = send(b23[1], "head", over[1])
    last = [b23, b3, rows_c[0], c1, c2, c3]
    return project(10 * DH, last, [half], half, final=True)


def solution(mesh):
    placed = (P("ctx", "head"), P("ctx", "head"), P("ctx", "head"), P(), P())
    return jax.shard_map(
        body, mesh=mesh, in_specs=placed, out_specs=P(("ctx", "head"), None), check_vma=False
    )
```

```python
import functools
import math

import jax
import jax.numpy as jnp
from jax import lax
from jax.experimental import pallas as pl
from jax.experimental.pallas import tpu as pltpu
from jax.sharding import PartitionSpec as P

DH = 128
HEADS_HERE = 4
GROUPS = ((0, 1), (2, 3))
PIECES = ((0, 1), (2,), (3,))
RES = 8
SUB = 16
BLK = RES * SUB
TAIL = 64
NEG = -1e30
RATE = math.log2(math.e) / math.sqrt(DH)
BF16 = jnp.bfloat16
F32 = jnp.float32
VMEM_LIMIT = 20 * 1024 * 1024


COST = {'mine0': 10**10, 'partner2': 10**10, 'lower': 3 * 10**9}


def iota(shape, dim):
    return lax.broadcasted_iota(jnp.int32, shape, dim)


def regroup_matrix(inverse):
    row, col = iota((BLK, BLK), 0), iota((BLK, BLK), 1)
    if inverse:
        hit = col == (row % RES) * SUB + row // RES
    else:
        hit = col == (row % SUB) * RES + row // SUB
    return jnp.where(hit, 1.0, 0.0).astype(BF16)


def causal_bias(position, size):
    rows = position(iota((size, size), 0))
    cols = position(iota((size, size), 1))
    return jnp.where(cols <= rows, 0.0, NEG)


def scores_of(q, blocks):
    scores = []
    for k, _, bias in blocks:
        s = lax.dot_general(q, k, (((1,), (1,)), ((), ())), preferred_element_type=F32)
        scores.append(s if bias is None else s + bias)
    return scores


def finish(scores, blocks):
    wide = scores[0]
    for s in scores[1:]:
        wide = jnp.maximum(wide, s)
    top = jnp.max(wide, axis=1, keepdims=True)
    total = None
    for s, (_, v, _) in zip(scores, blocks):
        p = jnp.exp2((s - top) * RATE).astype(BF16)
        with_ones = jnp.concatenate([v, jnp.ones(v.shape, BF16)], axis=1)
        part = jnp.dot(p, with_ones, preferred_element_type=F32)
        total = part if total is None else total + part
    row_sum = total[:, DH:]
    return total[:, :DH] / row_sum, top * RATE + jnp.log2(row_sum)


def attend_all(tasks):
    held = None
    for load, blocks, put in tasks:
        blocks = blocks()
        scores = scores_of(load(), blocks)
        if held is not None:
            held[2](*finish(held[0], held[1]))
        held = (scores, blocks, put)
    held[2](*finish(held[0], held[1]))


def merge(parts):
    top = parts[0][1]
    for _, lse in parts[1:]:
        top = jnp.maximum(top, lse)
    out, weight = 0.0, 0.0
    for o, lse in parts:
        w = jnp.exp2(lse - top)
        out += o * w
        weight += w
    return out / weight, top + jnp.log2(weight)


def add_rows(out, lse, at, part):
    held = out[at].shape
    was = (out[at].reshape(part[0].shape), lse[at].reshape(part[0].shape))
    o, s = merge([was, part])
    out[at] = o.reshape(held)
    lse[at] = s.reshape(held)


def rows_of(ref, level, shift, first=0, count=None):
    count = ref.shape[0] - first if count is None else count
    return [
        ref[pl.ds(first, count), shift + j * 2**level].reshape(count * SUB, DH)
        for j in range(RES // 2**level)
    ]


def shift_of(off_ref, level, head):
    return off_ref[level - 1, lax.axis_index("head") * HEADS_HERE + head]


def regroup(sources, targets):
    turn = regroup_matrix(False)
    heads, blocks = targets[0].shape[:2]
    for src, dst in zip(sources, targets):
        for b in range(blocks):
            x = src[b * BLK : (b + 1) * BLK, :]
            x = jnp.dot(turn, x, preferred_element_type=F32).astype(BF16)
            for h in range(heads):
                dst[h, b] = x[:, h * DH : (h + 1) * DH].reshape(RES, SUB, DH)


def prep_k_kernel(k_ref, kt):
    regroup((k_ref,), (kt,))


def prep_v_kernel(off_ref, v_ref, kt, vt, kv3, *kv2):
    regroup((v_ref,), (vt,))
    for h in range(kt.shape[0]):
        o2, o3 = (shift_of(off_ref, level, h) for level in (2, 3))
        (g,) = [g for g, members in enumerate(GROUPS) if h in members]
        n = GROUPS[g].index(h)
        for i, src in enumerate((kt, vt)):
            for j, x in enumerate(rows_of(src.at[h], 2, o2)):
                kv2[g][n, i, j] = x
            kv3[h, i] = rows_of(src.at[h], 3, o3)[0]


def prep_q_kernel(off_ref, q_ref, kt, vt, qt, first, q23):
    regroup((q_ref,), (qt,))
    for h in range(qt.shape[0]):
        o2, o3 = (shift_of(off_ref, level, h) for level in (2, 3))
        for j, x in enumerate(rows_of(qt.at[h], 2, o2) + rows_of(qt.at[h], 3, o3)):
            q23[h, j] = x

    @pl.when(lax.axis_index("ctx") % 2 == 1)
    def _():
        for h in range(2):
            for j, x in enumerate(rows_of(qt.at[h], 1, shift_of(off_ref, 1, h))):
                first[4 * h + j] = x

    @pl.when(lax.axis_index("ctx") % 2 == 0)
    def _():
        for i, src in enumerate((kt, vt)):
            for j, x in enumerate(rows_of(src.at[3], 1, shift_of(off_ref, 1, 3))):
                first[4 * i + j] = x


def own_kernel(heads, off_ref, qt, kt, vt, token, *outs):
    blocks = qt.shape[1]
    tasks = []

    def level0(h, n, step):
        head, out, lse = heads[h], outs[2 * h], outs[2 * h + 1]
        size = step * BLK
        bias = causal_bias(lambda r: r // BLK * BLK + r % SUB * RES + r % BLK // SUB, size)
        load = lambda ref, n: ref[head, n * step : (n + 1) * step].reshape(size, DH)

        def put(o, s):
            out[n * step : (n + 1) * step] = o.reshape(step, RES, SUB, DH)
            lse[n * step : (n + 1) * step] = s.reshape(step, RES, SUB, DH)

        tasks.append(
            (
                lambda: load(qt, n),
                lambda: [
                    (load(kt, i), load(vt, i), bias if i == n else None) for i in range(n + 1)
                ],
                put,
            )
        )

    def level1(h, n, step):
        head, out, lse = heads[h], outs[2 * h], outs[2 * h + 1]
        shift = shift_of(off_ref, 1, head)
        rows = step * SUB
        slices = RES // 2
        size = rows * slices
        bias = causal_bias(lambda r: r % rows * slices + r // rows, size)

        def load(ref, n):
            return jnp.concatenate(rows_of(ref.at[head], 1, shift, n * step, step), axis=0)

        def put(o, s):
            for j in range(slices):
                at = (pl.ds(n * step, step), shift + 2 * j)
                fresh = (o[j * rows : (j + 1) * rows], s[j * rows : (j + 1) * rows])
                add_rows(out, lse, at, fresh)

        tasks.append(
            (
                lambda: load(qt, n),
                lambda: [
                    (load(kt, i), load(vt, i), bias if i == n else None) for i in range(n + 1)
                ],
                put,
            )
        )

    for n in range(blocks // 2):
        for h in range(len(heads)):
            level0(h, n, 2)
    for n in range(blocks // 4):
        for h in range(len(heads)):
            level1(h, n, 4)
    attend_all(tasks)


def put_message(msg, slab, place, o, s, count):
    rows = o.shape[0] // count
    lane = iota((rows, DH), 1)
    for j in range(count):
        at = slice(j * rows, (j + 1) * rows)
        msg[(place + j) * rows : (place + j + 1) * rows, :] = o[at].astype(BF16)
        rest, now = s[at], slab[:rows, :]
        for i in range(3):
            piece = rest.astype(BF16)
            rest = rest - piece.astype(F32)
            now = jnp.where(lane == 3 * (place + j) + i, piece, now)
        slab[:rows, :] = now


def unit(rows):
    hit = iota((rows, DH), 0) == iota((rows, DH), 1)
    return jnp.where(hit, 1.0, 0.0).astype(BF16)


def close_message(msg, slab):
    first = msg.shape[0] - TAIL
    half = TAIL // 2
    turned = lax.dot_general(
        unit(half), slab[...], (((1,), (1,)), ((), ())), preferred_element_type=F32
    ).astype(BF16)
    for i in range(2):
        msg[first + i * half : first + (i + 1) * half, :] = turned[:, i * DH : (i + 1) * DH]


def open_message(msg, rows):
    first = msg.shape[0] - TAIL
    half = TAIL // 2
    parts = [
        lax.dot_general(
            msg[first + i * half : first + (i + 1) * half, :],
            unit(half),
            (((0,), (0,)), ((), ())),
            preferred_element_type=F32,
        )
        for i in range(2)
    ]
    return jnp.concatenate(parts, axis=0)[:rows]


def get_stat(slab, place):
    lane = iota(slab.shape, 1)
    hit = (lane >= 3 * place) & (lane < 3 * place + 3)
    return jnp.sum(jnp.where(hit, slab, 0.0), axis=1, keepdims=True)


def pair_tasks(load, keys, values, put):
    count = RES // 2

    def blocks():
        k, v = keys(), values()
        return [
            (jnp.concatenate(k[i : i + 2], axis=0), jnp.concatenate(v[i : i + 2], axis=0), None)
            for i in range(0, count, 2)
        ]

    return [
        (
            lambda j=j: jnp.concatenate(load()[j : j + 2], axis=0),
            blocks,
            lambda o, s, j=j: put(j, o, s),
        )
        for j in range(0, count, 2)
    ]


def lower_kernel(heads, off_ref, got, qt, kt, vt, token, msg, *refs):
    *local, slab = refs
    count = RES // 2
    rows = kt.shape[1] * SUB
    later = lax.axis_index("ctx") % 2 == 1
    msg[...] = jnp.zeros(msg.shape, BF16)
    slab[...] = jnp.zeros(slab.shape, BF16)

    @pl.when(jnp.logical_not(later))
    def _():
        tasks = []
        for n, head in enumerate(heads):
            shift = shift_of(off_ref, 1, head)
            tasks += pair_tasks(
                lambda n=n: [got[n * count + j] for j in range(count)],
                lambda head=head, shift=shift: rows_of(kt.at[head], 1, shift),
                lambda head=head, shift=shift: rows_of(vt.at[head], 1, shift),
                lambda j, o, s, n=n: put_message(msg, slab, n * count + j, o, s, 2),
            )
        attend_all(tasks)
        close_message(msg, slab)
        for ref, fill in zip(local, (0.0, NEG)):
            ref[...] = jnp.full(ref.shape, fill, F32)

    @pl.when(later)
    def _():
        for j, x in enumerate(rows_of(qt.at[2], 1, shift_of(off_ref, 1, 2))):
            msg[j * rows : (j + 1) * rows, :] = x
        shift = shift_of(off_ref, 1, 3)

        def put(j, o, s):
            for i in range(2):
                local[0][j + i] = o[i * rows : (i + 1) * rows]
                local[1][j + i] = s[i * rows : (i + 1) * rows]

        attend_all(
            pair_tasks(
                lambda: rows_of(qt.at[3], 1, shift),
                lambda: [got[j] for j in range(count)],
                lambda: [got[count + j] for j in range(count)],
                put,
            )
        )


def last_kernel(off_ref, turn, kt, vt, token, msg, slab):
    msg[...] = jnp.zeros(msg.shape, BF16)
    slab[...] = jnp.zeros(slab.shape, BF16)
    rows = kt.shape[1] * SUB

    @pl.when(lax.axis_index("ctx") % 2 == 0)
    def _():
        shift = shift_of(off_ref, 1, 2)
        attend_all(
            pair_tasks(
                lambda: [turn[j * rows : (j + 1) * rows, :] for j in range(RES // 2)],
                lambda: rows_of(kt.at[2], 1, shift),
                lambda: rows_of(vt.at[2], 1, shift),
                lambda j, o, s: put_message(msg, slab, j, o, s, 2),
            )
        )
        close_message(msg, slab)


def level_blocks(off_ref, level, head, n, kt, vt, kv2, near, far):
    ctx = lax.axis_index("ctx")
    z = ctx // 2
    shift = shift_of(off_ref, level, head)
    count = RES // 2**level
    rows = kt.shape[1] * SUB
    size = count * rows
    odd = jnp.where(z % 2 == 1, 0.0, NEG)
    high = jnp.where(z % 4 >= 2, 0.0, NEG)

    def whole(ref):
        return jnp.concatenate(rows_of(ref.at[head], level, shift), axis=0)

    def blocks(bias, which="all"):
        past = []
        if which != "own" and level == 2:
            past = [(kv2[n, 0].reshape(size, DH), kv2[n, 1].reshape(size, DH), odd)]
        elif which != "own":
            past = [
                (near[head, 0], near[head, 1], odd),
                (far[0, n, 0], far[0, n, 1], high),
                (far[1, n, 0], far[1, n, 1], high),
            ]
        return past if which == "past" else past + [(whole(kt), whole(vt), bias)]

    return whole, blocks, shift, count, rows


def partner_kernel(heads, off_ref, kt, vt, q23, kv2, near, far, token, *refs):
    later = jnp.where(lax.axis_index("ctx") % 2 == 0, 0.0, NEG)
    tasks = []
    msgs, slabs = refs[: len(refs) // 2], refs[len(refs) // 2 :]
    for slab in slabs:
        slab[...] = jnp.zeros(slab.shape, BF16)
    places = [0] * len(msgs)
    order = [(level, n) for level in (2, 3) for n in range(len(heads))]
    if len(msgs) > 1:
        order.sort(key=lambda item: item[1])
    for level, n in order:
        head, which = heads[n], n % len(msgs)
        _, blocks, _, count, rows = level_blocks(
            off_ref, level, head, n, kt, vt, kv2, near, far
        )
        first = 0 if level == 2 else 2
        tasks.append(
            (
                lambda h=head, f=first, c=count, r=rows: q23[h, f : f + c].reshape(c * r, DH),
                lambda blocks=blocks: blocks(later),
                lambda o, s, w=which, p=places[which], c=count: put_message(
                    msgs[w], slabs[w], p, o, s, c
                ),
            )
        )
        places[which] += count
    attend_all(tasks)
    for msg, slab in zip(msgs, slabs):
        close_message(msg, slab)


def add_message(msg, slab, place, out, lse, at, valid=None):
    rows = slab.shape[0]
    stat = get_stat(slab, place)
    if valid is not None:
        stat = jnp.where(valid, stat, NEG)
    part = msg[place * rows : (place + 1) * rows, :].astype(F32)
    add_rows(out, lse, at, (part, jnp.broadcast_to(stat, part.shape)))


def own_rows(heads, which, off_ref, qt, kt, vt, kv2, near, far, state):
    tasks = []
    for level in (2, 3):
        for n, head in enumerate(heads):
            out, lse = state[2 * n : 2 * n + 2]
            whole, blocks, shift, count, rows = level_blocks(
                off_ref, level, head, n, kt, vt, kv2, near, far
            )
            triangle = causal_bias(lambda r, c=count, m=rows: r % m * c + r // m, count * rows)

            def put(o, s, out=out, lse=lse, shift=shift, level=level, count=count, rows=rows):
                for j in range(count):
                    at = slice(j * rows, (j + 1) * rows)
                    add_rows(out, lse, (slice(None), shift + j * 2**level), (o[at], s[at]))

            tasks.append(
                (
                    lambda whole=whole: whole(qt),
                    lambda blocks=blocks, t=triangle: blocks(t, which),
                    put,
                )
            )
    attend_all(tasks)


def mine_kernel(heads, which, off_ref, *refs):
    number = len(heads)
    refs = refs[2 * number :]
    own_rows(heads, which, off_ref, *refs[:6], refs[7:])


def weights_kernel(off_ref, *refs):
    heads = GROUPS[1]
    number = len(heads)
    qt, kt, vt, o1, s1, w_ref, token, *refs = refs[2 * number :]
    state, out = refs[:-1], refs[-1]
    mine = lax.axis_index("head")
    at = 0
    for members in PIECES:
        width = len(members) * DH
        for t in range(4):
            first = (mine ^ t) * (HEADS_HERE * DH) + members[0] * DH
            out[at : at + width, :] = w_ref[pl.ds(pl.multiple_of(first, DH), width), :]
            at += width
    own_rows(heads, "own", off_ref, qt, kt, vt, None, None, None, state)
    for j in range(RES // 2):
        at = (slice(None), shift_of(off_ref, 1, 3) + 2 * j)
        add_rows(state[-2], state[-1], at, (o1[j], s1[j]))


def finish_kernel(heads, stacked, off_ref, *refs):
    number = len(heads)
    refs = refs[2 * number :]
    msg, token, *below = refs[: -4 - 2 * number]
    dests, state = refs[-4 - 2 * number : -2 * number], refs[-2 * number :]
    rows = state[0].shape[0] * SUB
    later = lax.axis_index("ctx") % 2 == 1
    if below:
        slab = open_message(below[0], rows)
        for n, head in enumerate(heads):
            for j in range(RES // 2):
                at = (slice(None), shift_of(off_ref, 1, head) + 2 * j)
                place = n * (RES // 2) + j
                add_message(below[0], slab, place, state[2 * n], state[2 * n + 1], at, later)
    slab = open_message(msg, rows)
    place = 0
    for level in (2, 3):
        for n, head in enumerate(heads):
            shift = shift_of(off_ref, level, head)
            for j in range(RES // 2**level):
                at = (slice(None), shift + j * 2**level)
                add_message(msg, slab, place, state[2 * n], state[2 * n + 1], at)
                place += 1
    mine = lax.axis_index("head")
    per = state[0].shape[0] // 4
    if stacked:
        dests = (dests[0], dests[1], dests[2].at[0], dests[2].at[1])
    for t, dest in enumerate(dests):
        for n in range(number):
            x = state[2 * n][pl.ds((mine ^ t) * per, per)].reshape(per * BLK, DH)
            dest[:, n * DH : (n + 1) * DH] = x.astype(BF16)


def project_kernel(first, added, final, *refs):
    if final:
        *pieces, w_ref, token, out_hbm, plain, out, sems = refs
    else:
        *pieces, w_ref, token, out, plain = refs
    if added:
        *pieces, before = pieces
    back = regroup_matrix(True)
    depth = plain.shape[1]
    for b in range(plain.shape[0] // BLK):
        rows = slice(b * BLK, (b + 1) * BLK)
        x = jnp.concatenate(
            [src[0, rows, :] if len(src.shape) == 3 else src[rows, :] for src in pieces], axis=1
        )
        plain[rows, :] = jnp.dot(back, x, preferred_element_type=F32).astype(BF16)
    tile = 1024
    steps = out.shape[1] // tile

    def copy(step):
        cols = pl.ds(pl.multiple_of(step * tile, tile), tile)
        return pltpu.make_async_copy(out.at[:, cols], out_hbm.at[:, cols], sems.at[step])

    @pl.loop(0, steps)
    def _(step):
        cols = pl.ds(pl.multiple_of(step * tile, tile), tile)
        total = jnp.dot(
            plain[...], w_ref[first : first + depth, cols], preferred_element_type=F32
        )
        if added:
            total = total + before[:, cols]
        out[:, cols] = total.astype(out.dtype)
        if final:
            copy(step).start()

    if final:

        @pl.loop(0, steps)
        def _(step):
            copy(step).wait()


SMEM = pl.BlockSpec(memory_space=pltpu.SMEM)
VMEM = pl.BlockSpec(memory_space=pltpu.VMEM)
ANY = pl.BlockSpec(memory_space=pl.ANY)


def shape(*dims, dtype=BF16):
    return jax.ShapeDtypeStruct(dims, dtype)


def call(kernel, specs, outs, name, scratch=(), aliases={}, out_spec=VMEM):
    return pl.pallas_call(
        kernel,
        in_specs=specs,
        out_specs=jax.tree.map(lambda _: out_spec, outs),
        out_shape=outs,
        scratch_shapes=scratch,
        input_output_aliases=aliases,
        compiler_params=pltpu.CompilerParams(vmem_limit_bytes=VMEM_LIMIT),
        cost_estimate=pl.CostEstimate(flops=COST.get(name, 10**9), bytes_accessed=1, transcendentals=0),
        name=name,
    )


def body(queries, keys, values, offsets, out_weight):
    rows_here, width = queries.shape
    blocks = rows_here // BLK
    heads = width // DH
    slots = rows_here // RES
    piece = (slots, DH)
    message = lambda count: shape(count * slots + TAIL, DH)
    slab = pltpu.VMEM((2 * DH, DH), BF16)
    regrouped = shape(heads, blocks, RES, SUB, DH)
    ctx_size = lax.axis_size("ctx")
    swap = [(i, i ^ 1) for i in range(ctx_size)]
    near = [(i, i ^ 2) for i in range(ctx_size)]
    far = [(i, i ^ 4) for i in range(ctx_size)]
    over = [[(i, i ^ t) for i in range(4)] for t in range(4)]

    kt = call(prep_k_kernel, [VMEM], regrouped, "prep_k")(keys)
    vt, kv3, *kv2 = call(
        prep_v_kernel,
        [SMEM, VMEM, VMEM],
        [regrouped, shape(heads, 2, *piece)]
        + [shape(len(members), 2, 2, *piece) for members in GROUPS],
        "prep_v",
    )(offsets, values, kt)
    kv3_near = lax.ppermute(kv3, "ctx", near)
    qt, first, q23 = call(
        prep_q_kernel,
        [SMEM, VMEM, VMEM, VMEM],
        [regrouped, shape(8, *piece), shape(heads, 3, *piece)],
        "prep_q",
    )(offsets, queries, kt, vt)
    first = lax.ppermute(first, "ctx", swap)

    state = shape(blocks, RES, SUB, DH, dtype=F32)

    def own(members, token):
        return call(
            functools.partial(own_kernel, members),
            [SMEM, VMEM, VMEM, VMEM, ANY],
            [state] * (2 * len(members)),
            "own%d" % members[0],
        )(offsets, qt, kt, vt, token)

    def lower(members, got, token):
        return call(
            functools.partial(lower_kernel, members),
            [SMEM] + [VMEM] * 4 + [ANY],
            [message(len(members) * 4)] + [shape(4, *piece, dtype=F32)] * 2,
            "lower",
            scratch=[slab],
        )(offsets, got, qt, kt, vt, token)

    def partner(members, column, token, messages):
        return call(
            functools.partial(partner_kernel, members),
            [SMEM] + [VMEM] * 6 + [ANY],
            [message(len(members) // messages * 3)] * messages,
            "partner%d" % members[0],
            scratch=[slab] * messages,
        )(offsets, kt, vt, q23, *column, token)

    def mine(members, rows, column, token, which="all"):
        return call(
            functools.partial(mine_kernel, members, which),
            [SMEM] + [VMEM] * (len(rows) + 6) + [ANY],
            [state] * len(rows),
            "mine%d" % members[0],
            aliases={1 + i: i for i in range(len(rows))},
        )(offsets, *rows, qt, kt, vt, *column, token)

    def finished(members, rows, message, token, *below):
        dest = shape(rows_here // 4, len(members) * DH)
        stacked = members != PIECES[-1]
        dests = [dest, dest, shape(2, *dest.shape), shape(8, DH)] if stacked else [dest] * 4
        return call(
            functools.partial(finish_kernel, members, stacked),
            [SMEM] + [VMEM] * (len(rows) + 1) + [ANY] + [VMEM] * len(below),
            dests + [state] * len(rows),
            "finish%d" % members[0],
            aliases={1 + i: 4 + i for i in range(len(rows))},
        )(offsets, *rows, message, token, *below)[:4]

    def project(first, pieces, before, token, final=False):
        model = out_weight.shape[1]
        total = shape(rows_here // 4, model, dtype=BF16 if final else F32)
        scratch = [pltpu.VMEM((rows_here // 4, sum(x.shape[-1] for x in pieces)), BF16)]
        if final:
            scratch += [
                pltpu.VMEM((rows_here // 4, model), BF16),
                pltpu.SemaphoreType.DMA((model // 1024,)),
            ]
        return call(
            functools.partial(project_kernel, first, len(before), final),
            [VMEM] * (len(pieces) + 1 + len(before)) + [ANY],
            total,
            "project%d" % first,
            scratch=scratch,
            out_spec=ANY if final else VMEM,
        )(*pieces, *before, weights, token)

    def both(members):
        cut = slice(members[0], members[-1] + 1)
        return jnp.stack([kv3[cut], kv3_near[cut]])

    def send(value, axis, pairs):
        return lax.ppermute(value, axis, pairs)

    group_a, group_b = GROUPS
    *rows_a, = own((0, 1), kv3)
    kv3_near, rows_a[1] = lax.optimization_barrier((kv3_near, rows_a[1]))
    far_a, kv2_a, q23 = lax.optimization_barrier((both(group_a), kv2[0], q23))
    rows_b = own((2, 3), far_a)
    far_a, kv2_a = send(far_a, "ctx", far), send(kv2_a, "ctx", near)
    q23 = send(q23, "ctx", swap)
    msg1, o1, s1 = lower((0, 1), first, rows_b[0])
    turn = send(msg1, "ctx", swap)
    *rows_b, weights = call(
        weights_kernel,
        [SMEM] + [VMEM] * 10 + [ANY],
        [state] * 4 + [shape(*out_weight.shape)],
        "weights",
        aliases={1 + i: i for i in range(4)},
    )(offsets, *rows_b, qt, kt, vt, o1, s1, out_weight, msg1)

    far_a, kv2_a, far_b, kv2_b, weights = lax.optimization_barrier(
        (far_a, kv2_a, both(group_b), kv2[1], weights)
    )
    ready = far_b
    far_b, kv2_b = send(far_b, "ctx", far), send(kv2_b, "ctx", near)
    column_a = [kv2_a, kv3_near, far_a]
    (msg_a,) = partner(group_a, column_a, ready, 1)
    got_a = send(msg_a, "ctx", swap)
    rows_a = list(mine(group_a, rows_a, column_a, msg_a))
    msg1c = call(
        last_kernel,
        [SMEM] + [VMEM] * 3 + [ANY],
        message(RES // 2),
        "last",
        scratch=[slab],
    )(offsets, turn, kt, vt, rows_a[0])
    got1c = send(msg1c, "ctx", swap)
    rows_a = finished(group_a, rows_a, got_a, msg1c, turn)
    a1, a23 = send(rows_a[1], "head", over[1]), send(rows_a[2], "head", over[2])

    column_b = [kv2_b, kv3_near, far_b]
    msg_b, msg_c = partner(group_b, column_b, rows_a[0], 2)
    got_b, got_c = send(msg_b, "ctx", swap), send(msg_c, "ctx", swap)
    rows_b = mine(group_b, rows_b, column_b, msg_c, "past")
    a23, *rows_b = lax.optimization_barrier((a23, *rows_b))
    a3 = send(a23[1], "head", over[1])
    rows_b, rows_c = rows_b[:2], rows_b[2:]
    rows_b = finished((2,), rows_b, got_b, rows_c[0], got1c)
    b1, b23 = send(rows_b[1], "head", over[1]), send(rows_b[2], "head", over[2])
    rows_c = finished((3,), rows_c, got_c, rows_b[0])
    c2, c3, c1 = (send(rows_c[t], "head", over[t]) for t in (2, 3, 1))
    half = project(0, [rows_a[0], a1, a23, a3, rows_b[0], b1], [], rows_c[0])
    b23, half = lax.optimization_barrier((b23, half))
    b3 = send(b23[1], "head", over[1])
    last = [b23, b3, rows_c[0], c1, c2, c3]
    return project(10 * DH, last, [half], half, final=True)


def solution(mesh):
    placed = (P("ctx", "head"), P("ctx", "head"), P("ctx", "head"), P(), P())
    return jax.shard_map(
        body, mesh=mesh, in_specs=placed, out_specs=P(("ctx", "head"), None), check_vma=False
    )
```

```python
import functools
import math

import jax
import jax.numpy as jnp
from jax import lax
from jax.experimental import pallas as pl
from jax.experimental.pallas import tpu as pltpu
from jax.sharding import PartitionSpec as P

DH = 128
HEADS_HERE = 4
GROUPS = ((0, 1), (2, 3))
PIECES = ((0, 1), (2,), (3,))
RES = 8
SUB = 16
BLK = RES * SUB
TAIL = 64
NEG = -1e30
RATE = math.log2(math.e) / math.sqrt(DH)
BF16 = jnp.bfloat16
F32 = jnp.float32
VMEM_LIMIT = 20 * 1024 * 1024


COST = {'mine0': 10**10, 'partner2': 10**10, 'lower': 3 * 10**9}


def iota(shape, dim):
    return lax.broadcasted_iota(jnp.int32, shape, dim)


def regroup_matrix(inverse):
    row, col = iota((BLK, BLK), 0), iota((BLK, BLK), 1)
    if inverse:
        hit = col == (row % RES) * SUB + row // RES
    else:
        hit = col == (row % SUB) * RES + row // SUB
    return jnp.where(hit, 1.0, 0.0).astype(BF16)


def causal_bias(position, size):
    rows = position(iota((size, size), 0))
    cols = position(iota((size, size), 1))
    return jnp.where(cols <= rows, 0.0, NEG)


def scores_of(q, blocks):
    scores = []
    for k, _, bias in blocks:
        s = lax.dot_general(q, k, (((1,), (1,)), ((), ())), preferred_element_type=F32)
        scores.append(s if bias is None else s + bias)
    return scores


def finish(scores, blocks):
    wide = scores[0]
    for s in scores[1:]:
        wide = jnp.maximum(wide, s)
    top = jnp.max(wide, axis=1, keepdims=True)
    total = None
    for s, (_, v, _) in zip(scores, blocks):
        p = jnp.exp2((s - top) * RATE).astype(BF16)
        with_ones = jnp.concatenate([v, jnp.ones(v.shape, BF16)], axis=1)
        part = jnp.dot(p, with_ones, preferred_element_type=F32)
        total = part if total is None else total + part
    row_sum = total[:, DH:]
    return total[:, :DH] / row_sum, top * RATE + jnp.log2(row_sum)


def attend_all(tasks):
    held = None
    for load, blocks, put in tasks:
        blocks = blocks()
        scores = scores_of(load(), blocks)
        if held is not None:
            held[2](*finish(held[0], held[1]))
        held = (scores, blocks, put)
    held[2](*finish(held[0], held[1]))


def merge(parts):
    top = parts[0][1]
    for _, lse in parts[1:]:
        top = jnp.maximum(top, lse)
    out, weight = 0.0, 0.0
    for o, lse in parts:
        w = jnp.exp2(lse - top)
        out += o * w
        weight += w
    return out / weight, top + jnp.log2(weight)


def add_rows(out, lse, at, part):
    held = out[at].shape
    was = (out[at].reshape(part[0].shape), lse[at].reshape(part[0].shape))
    o, s = merge([was, part])
    out[at] = o.reshape(held)
    lse[at] = s.reshape(held)


def rows_of(ref, level, shift, first=0, count=None):
    count = ref.shape[0] - first if count is None else count
    return [
        ref[pl.ds(first, count), shift + j * 2**level].reshape(count * SUB, DH)
        for j in range(RES // 2**level)
    ]


def shift_of(off_ref, level, head):
    return off_ref[level - 1, lax.axis_index("head") * HEADS_HERE + head]


def regroup(sources, targets):
    turn = regroup_matrix(False)
    heads, blocks = targets[0].shape[:2]
    for src, dst in zip(sources, targets):
        for b in range(blocks):
            x = src[b * BLK : (b + 1) * BLK, :]
            x = jnp.dot(turn, x, preferred_element_type=F32).astype(BF16)
            for h in range(heads):
                dst[h, b] = x[:, h * DH : (h + 1) * DH].reshape(RES, SUB, DH)


def prep_k_kernel(k_ref, kt):
    regroup((k_ref,), (kt,))


def prep_v_kernel(off_ref, v_ref, kt, vt, kv3, *kv2):
    regroup((v_ref,), (vt,))
    for h in range(kt.shape[0]):
        o2, o3 = (shift_of(off_ref, level, h) for level in (2, 3))
        (g,) = [g for g, members in enumerate(GROUPS) if h in members]
        n = GROUPS[g].index(h)
        for i, src in enumerate((kt, vt)):
            for j, x in enumerate(rows_of(src.at[h], 2, o2)):
                kv2[g][n, i, j] = x
            kv3[h, i] = rows_of(src.at[h], 3, o3)[0]


def prep_q_kernel(off_ref, q_ref, kt, vt, qt, first, q23):
    regroup((q_ref,), (qt,))
    for h in range(qt.shape[0]):
        o2, o3 = (shift_of(off_ref, level, h) for level in (2, 3))
        for j, x in enumerate(rows_of(qt.at[h], 2, o2) + rows_of(qt.at[h], 3, o3)):
            q23[h, j] = x

    @pl.when(lax.axis_index("ctx") % 2 == 1)
    def _():
        for h in range(2):
            for j, x in enumerate(rows_of(qt.at[h], 1, shift_of(off_ref, 1, h))):
                first[4 * h + j] = x

    @pl.when(lax.axis_index("ctx") % 2 == 0)
    def _():
        for i, src in enumerate((kt, vt)):
            for j, x in enumerate(rows_of(src.at[3], 1, shift_of(off_ref, 1, 3))):
                first[4 * i + j] = x


def own_kernel(heads, off_ref, qt, kt, vt, token, *outs):
    blocks = qt.shape[1]
    tasks = []

    def level0(h, n, step):
        head, out, lse = heads[h], outs[2 * h], outs[2 * h + 1]
        size = step * BLK
        bias = causal_bias(lambda r: r // BLK * BLK + r % SUB * RES + r % BLK // SUB, size)
        load = lambda ref, n: ref[head, n * step : (n + 1) * step].reshape(size, DH)

        def put(o, s):
            out[n * step : (n + 1) * step] = o.reshape(step, RES, SUB, DH)
            lse[n * step : (n + 1) * step] = s.reshape(step, RES, SUB, DH)

        tasks.append(
            (
                lambda: load(qt, n),
                lambda: [
                    (load(kt, i), load(vt, i), bias if i == n else None) for i in range(n + 1)
                ],
                put,
            )
        )

    def level1(h, n, step):
        head, out, lse = heads[h], outs[2 * h], outs[2 * h + 1]
        shift = shift_of(off_ref, 1, head)
        rows = step * SUB
        slices = RES // 2
        size = rows * slices
        bias = causal_bias(lambda r: r % rows * slices + r // rows, size)

        def load(ref, n):
            return jnp.concatenate(rows_of(ref.at[head], 1, shift, n * step, step), axis=0)

        def put(o, s):
            for j in range(slices):
                at = (pl.ds(n * step, step), shift + 2 * j)
                fresh = (o[j * rows : (j + 1) * rows], s[j * rows : (j + 1) * rows])
                add_rows(out, lse, at, fresh)

        tasks.append(
            (
                lambda: load(qt, n),
                lambda: [
                    (load(kt, i), load(vt, i), bias if i == n else None) for i in range(n + 1)
                ],
                put,
            )
        )

    for n in range(blocks // 2):
        for h in range(len(heads)):
            level0(h, n, 2)
    for n in range(blocks // 4):
        for h in range(len(heads)):
            level1(h, n, 4)
    attend_all(tasks)


def put_message(msg, slab, place, o, s, count):
    rows = o.shape[0] // count
    lane = iota((rows, DH), 1)
    for j in range(count):
        at = slice(j * rows, (j + 1) * rows)
        msg[(place + j) * rows : (place + j + 1) * rows, :] = o[at].astype(BF16)
        rest, now = s[at], slab[:rows, :]
        for i in range(3):
            piece = rest.astype(BF16)
            rest = rest - piece.astype(F32)
            now = jnp.where(lane == 3 * (place + j) + i, piece, now)
        slab[:rows, :] = now


def unit(rows):
    hit = iota((rows, DH), 0) == iota((rows, DH), 1)
    return jnp.where(hit, 1.0, 0.0).astype(BF16)


def close_message(msg, slab):
    first = msg.shape[0] - TAIL
    half = TAIL // 2
    turned = lax.dot_general(
        unit(half), slab[...], (((1,), (1,)), ((), ())), preferred_element_type=F32
    ).astype(BF16)
    for i in range(2):
        msg[first + i * half : first + (i + 1) * half, :] = turned[:, i * DH : (i + 1) * DH]


def open_message(msg, rows):
    first = msg.shape[0] - TAIL
    half = TAIL // 2
    parts = [
        lax.dot_general(
            msg[first + i * half : first + (i + 1) * half, :],
            unit(half),
            (((0,), (0,)), ((), ())),
            preferred_element_type=F32,
        )
        for i in range(2)
    ]
    return jnp.concatenate(parts, axis=0)[:rows]


def get_stat(slab, place):
    lane = iota(slab.shape, 1)
    hit = (lane >= 3 * place) & (lane < 3 * place + 3)
    return jnp.sum(jnp.where(hit, slab, 0.0), axis=1, keepdims=True)


def pair_tasks(load, keys, values, put):
    count = RES // 2

    def blocks():
        k, v = keys(), values()
        return [
            (jnp.concatenate(k[i : i + 2], axis=0), jnp.concatenate(v[i : i + 2], axis=0), None)
            for i in range(0, count, 2)
        ]

    return [
        (
            lambda j=j: jnp.concatenate(load()[j : j + 2], axis=0),
            blocks,
            lambda o, s, j=j: put(j, o, s),
        )
        for j in range(0, count, 2)
    ]


def lower_kernel(heads, off_ref, got, qt, kt, vt, token, msg, *refs):
    *local, slab = refs
    count = RES // 2
    rows = kt.shape[1] * SUB
    later = lax.axis_index("ctx") % 2 == 1
    msg[...] = jnp.zeros(msg.shape, BF16)
    slab[...] = jnp.zeros(slab.shape, BF16)

    @pl.when(jnp.logical_not(later))
    def _():
        tasks = []
        for n, head in enumerate(heads):
            shift = shift_of(off_ref, 1, head)
            tasks += pair_tasks(
                lambda n=n: [got[n * count + j] for j in range(count)],
                lambda head=head, shift=shift: rows_of(kt.at[head], 1, shift),
                lambda head=head, shift=shift: rows_of(vt.at[head], 1, shift),
                lambda j, o, s, n=n: put_message(msg, slab, n * count + j, o, s, 2),
            )
        attend_all(tasks)
        close_message(msg, slab)
        for ref, fill in zip(local, (0.0, NEG)):
            ref[...] = jnp.full(ref.shape, fill, F32)

    @pl.when(later)
    def _():
        for j, x in enumerate(rows_of(qt.at[2], 1, shift_of(off_ref, 1, 2))):
            msg[j * rows : (j + 1) * rows, :] = x
        shift = shift_of(off_ref, 1, 3)

        def put(j, o, s):
            for i in range(2):
                local[0][j + i] = o[i * rows : (i + 1) * rows]
                local[1][j + i] = s[i * rows : (i + 1) * rows]

        attend_all(
            pair_tasks(
                lambda: rows_of(qt.at[3], 1, shift),
                lambda: [got[j] for j in range(count)],
                lambda: [got[count + j] for j in range(count)],
                put,
            )
        )


def last_kernel(off_ref, turn, kt, vt, token, msg, slab):
    msg[...] = jnp.zeros(msg.shape, BF16)
    slab[...] = jnp.zeros(slab.shape, BF16)
    rows = kt.shape[1] * SUB

    @pl.when(lax.axis_index("ctx") % 2 == 0)
    def _():
        shift = shift_of(off_ref, 1, 2)
        attend_all(
            pair_tasks(
                lambda: [turn[j * rows : (j + 1) * rows, :] for j in range(RES // 2)],
                lambda: rows_of(kt.at[2], 1, shift),
                lambda: rows_of(vt.at[2], 1, shift),
                lambda j, o, s: put_message(msg, slab, j, o, s, 2),
            )
        )
        close_message(msg, slab)


def level_blocks(off_ref, level, head, n, kt, vt, kv2, near, far):
    ctx = lax.axis_index("ctx")
    z = ctx // 2
    shift = shift_of(off_ref, level, head)
    count = RES // 2**level
    rows = kt.shape[1] * SUB
    size = count * rows
    odd = jnp.where(z % 2 == 1, 0.0, NEG)
    high = jnp.where(z % 4 >= 2, 0.0, NEG)

    def whole(ref):
        return jnp.concatenate(rows_of(ref.at[head], level, shift), axis=0)

    def blocks(bias, which="all"):
        past = []
        if which != "own" and level == 2:
            past = [(kv2[n, 0].reshape(size, DH), kv2[n, 1].reshape(size, DH), odd)]
        elif which != "own":
            past = [
                (near[head, 0], near[head, 1], odd),
                (far[0, n, 0], far[0, n, 1], high),
                (far[1, n, 0], far[1, n, 1], high),
            ]
        return past if which == "past" else past + [(whole(kt), whole(vt), bias)]

    return whole, blocks, shift, count, rows


def partner_kernel(heads, off_ref, kt, vt, q23, kv2, near, far, token, *refs):
    later = jnp.where(lax.axis_index("ctx") % 2 == 0, 0.0, NEG)
    tasks = []
    msgs, slabs = refs[: len(refs) // 2], refs[len(refs) // 2 :]
    for slab in slabs:
        slab[...] = jnp.zeros(slab.shape, BF16)
    places = [0] * len(msgs)
    order = [(level, n) for level in (2, 3) for n in range(len(heads))]
    if len(msgs) > 1:
        order.sort(key=lambda item: item[1])
    for level, n in order:
        head, which = heads[n], n % len(msgs)
        _, blocks, _, count, rows = level_blocks(
            off_ref, level, head, n, kt, vt, kv2, near, far
        )
        first = 0 if level == 2 else 2
        tasks.append(
            (
                lambda h=head, f=first, c=count, r=rows: q23[h, f : f + c].reshape(c * r, DH),
                lambda blocks=blocks: blocks(later),
                lambda o, s, w=which, p=places[which], c=count: put_message(
                    msgs[w], slabs[w], p, o, s, c
                ),
            )
        )
        places[which] += count
    attend_all(tasks)
    for msg, slab in zip(msgs, slabs):
        close_message(msg, slab)


def add_message(msg, slab, place, out, lse, at, valid=None):
    rows = slab.shape[0]
    stat = get_stat(slab, place)
    if valid is not None:
        stat = jnp.where(valid, stat, NEG)
    part = msg[place * rows : (place + 1) * rows, :].astype(F32)
    add_rows(out, lse, at, (part, jnp.broadcast_to(stat, part.shape)))


def own_rows(heads, which, off_ref, qt, kt, vt, kv2, near, far, state):
    tasks = []
    for level in (2, 3):
        for n, head in enumerate(heads):
            out, lse = state[2 * n : 2 * n + 2]
            whole, blocks, shift, count, rows = level_blocks(
                off_ref, level, head, n, kt, vt, kv2, near, far
            )
            triangle = causal_bias(lambda r, c=count, m=rows: r % m * c + r // m, count * rows)

            def put(o, s, out=out, lse=lse, shift=shift, level=level, count=count, rows=rows):
                for j in range(count):
                    at = slice(j * rows, (j + 1) * rows)
                    add_rows(out, lse, (slice(None), shift + j * 2**level), (o[at], s[at]))

            tasks.append(
                (
                    lambda whole=whole: whole(qt),
                    lambda blocks=blocks, t=triangle: blocks(t, which),
                    put,
                )
            )
    attend_all(tasks)


def mine_kernel(heads, which, off_ref, *refs):
    number = len(heads)
    refs = refs[2 * number :]
    own_rows(heads, which, off_ref, *refs[:6], refs[7:])


def weights_kernel(off_ref, *refs):
    heads = GROUPS[1]
    number = len(heads)
    qt, kt, vt, o1, s1, w_ref, token, *refs = refs[2 * number :]
    state, out = refs[:-1], refs[-1]
    mine = lax.axis_index("head")
    at = 0
    for members in PIECES:
        width = len(members) * DH
        for t in range(4):
            first = (mine ^ t) * (HEADS_HERE * DH) + members[0] * DH
            out[at : at + width, :] = w_ref[pl.ds(pl.multiple_of(first, DH), width), :]
            at += width
    own_rows(heads, "own", off_ref, qt, kt, vt, None, None, None, state)
    for j in range(RES // 2):
        at = (slice(None), shift_of(off_ref, 1, 3) + 2 * j)
        add_rows(state[-2], state[-1], at, (o1[j], s1[j]))


def finish_kernel(heads, stacked, off_ref, *refs):
    number = len(heads)
    refs = refs[2 * number :]
    msg, token, *below = refs[: -4 - 2 * number]
    dests, state = refs[-4 - 2 * number : -2 * number], refs[-2 * number :]
    rows = state[0].shape[0] * SUB
    later = lax.axis_index("ctx") % 2 == 1
    if below:
        slab = open_message(below[0], rows)
        for n, head in enumerate(heads):
            for j in range(RES // 2):
                at = (slice(None), shift_of(off_ref, 1, head) + 2 * j)
                place = n * (RES // 2) + j
                add_message(below[0], slab, place, state[2 * n], state[2 * n + 1], at, later)
    slab = open_message(msg, rows)
    place = 0
    for level in (2, 3):
        for n, head in enumerate(heads):
            shift = shift_of(off_ref, level, head)
            for j in range(RES // 2**level):
                at = (slice(None), shift + j * 2**level)
                add_message(msg, slab, place, state[2 * n], state[2 * n + 1], at)
                place += 1
    mine = lax.axis_index("head")
    per = state[0].shape[0] // 4
    if stacked:
        dests = (dests[0], dests[1], dests[2].at[0], dests[2].at[1])
    for t, dest in enumerate(dests):
        for n in range(number):
            x = state[2 * n][pl.ds((mine ^ t) * per, per)].reshape(per * BLK, DH)
            dest[:, n * DH : (n + 1) * DH] = x.astype(BF16)


def project_kernel(first, added, final, *refs):
    if final:
        *pieces, w_ref, token, out_hbm, plain, out, sems = refs
    else:
        *pieces, w_ref, token, out, plain = refs
    if added:
        *pieces, before = pieces
    back = regroup_matrix(True)
    depth = plain.shape[1]
    for b in range(plain.shape[0] // BLK):
        rows = slice(b * BLK, (b + 1) * BLK)
        x = jnp.concatenate(
            [src[0, rows, :] if len(src.shape) == 3 else src[rows, :] for src in pieces], axis=1
        )
        plain[rows, :] = jnp.dot(back, x, preferred_element_type=F32).astype(BF16)
    tile = 512
    steps = out.shape[1] // tile

    def copy(step):
        cols = pl.ds(step * tile, tile)
        return pltpu.make_async_copy(out.at[:, cols], out_hbm.at[:, cols], sems.at[step])

    for step in range(steps):
        cols = pl.ds(step * tile, tile)
        total = jnp.dot(
            plain[...], w_ref[first : first + depth, cols], preferred_element_type=F32
        )
        if added:
            total = total + before[:, cols]
        out[:, cols] = total.astype(out.dtype)
        if final:
            copy(step).start()

    if final:
        for step in range(steps):
            copy(step).wait()


SMEM = pl.BlockSpec(memory_space=pltpu.SMEM)
VMEM = pl.BlockSpec(memory_space=pltpu.VMEM)
ANY = pl.BlockSpec(memory_space=pl.ANY)


def shape(*dims, dtype=BF16):
    return jax.ShapeDtypeStruct(dims, dtype)


def call(kernel, specs, outs, name, scratch=(), aliases={}, out_spec=VMEM):
    return pl.pallas_call(
        kernel,
        in_specs=specs,
        out_specs=jax.tree.map(lambda _: out_spec, outs),
        out_shape=outs,
        scratch_shapes=scratch,
        input_output_aliases=aliases,
        compiler_params=pltpu.CompilerParams(vmem_limit_bytes=VMEM_LIMIT),
        cost_estimate=pl.CostEstimate(flops=COST.get(name, 10**9), bytes_accessed=1, transcendentals=0),
        name=name,
    )


def body(queries, keys, values, offsets, out_weight):
    rows_here, width = queries.shape
    blocks = rows_here // BLK
    heads = width // DH
    slots = rows_here // RES
    piece = (slots, DH)
    message = lambda count: shape(count * slots + TAIL, DH)
    slab = pltpu.VMEM((2 * DH, DH), BF16)
    regrouped = shape(heads, blocks, RES, SUB, DH)
    ctx_size = lax.axis_size("ctx")
    swap = [(i, i ^ 1) for i in range(ctx_size)]
    near = [(i, i ^ 2) for i in range(ctx_size)]
    far = [(i, i ^ 4) for i in range(ctx_size)]
    over = [[(i, i ^ t) for i in range(4)] for t in range(4)]

    kt = call(prep_k_kernel, [VMEM], regrouped, "prep_k")(keys)
    vt, kv3, *kv2 = call(
        prep_v_kernel,
        [SMEM, VMEM, VMEM],
        [regrouped, shape(heads, 2, *piece)]
        + [shape(len(members), 2, 2, *piece) for members in GROUPS],
        "prep_v",
    )(offsets, values, kt)
    kv3_near = lax.ppermute(kv3, "ctx", near)
    qt, first, q23 = call(
        prep_q_kernel,
        [SMEM, VMEM, VMEM, VMEM],
        [regrouped, shape(8, *piece), shape(heads, 3, *piece)],
        "prep_q",
    )(offsets, queries, kt, vt)
    first = lax.ppermute(first, "ctx", swap)

    state = shape(blocks, RES, SUB, DH, dtype=F32)

    def own(members, token):
        return call(
            functools.partial(own_kernel, members),
            [SMEM, VMEM, VMEM, VMEM, ANY],
            [state] * (2 * len(members)),
            "own%d" % members[0],
        )(offsets, qt, kt, vt, token)

    def lower(members, got, token):
        return call(
            functools.partial(lower_kernel, members),
            [SMEM] + [VMEM] * 4 + [ANY],
            [message(len(members) * 4)] + [shape(4, *piece, dtype=F32)] * 2,
            "lower",
            scratch=[slab],
        )(offsets, got, qt, kt, vt, token)

    def partner(members, column, token, messages):
        return call(
            functools.partial(partner_kernel, members),
            [SMEM] + [VMEM] * 6 + [ANY],
            [message(len(members) // messages * 3)] * messages,
            "partner%d" % members[0],
            scratch=[slab] * messages,
        )(offsets, kt, vt, q23, *column, token)

    def mine(members, rows, column, token, which="all"):
        return call(
            functools.partial(mine_kernel, members, which),
            [SMEM] + [VMEM] * (len(rows) + 6) + [ANY],
            [state] * len(rows),
            "mine%d" % members[0],
            aliases={1 + i: i for i in range(len(rows))},
        )(offsets, *rows, qt, kt, vt, *column, token)

    def finished(members, rows, message, token, *below):
        dest = shape(rows_here // 4, len(members) * DH)
        stacked = members != PIECES[-1]
        dests = [dest, dest, shape(2, *dest.shape), shape(8, DH)] if stacked else [dest] * 4
        return call(
            functools.partial(finish_kernel, members, stacked),
            [SMEM] + [VMEM] * (len(rows) + 1) + [ANY] + [VMEM] * len(below),
            dests + [state] * len(rows),
            "finish%d" % members[0],
            aliases={1 + i: 4 + i for i in range(len(rows))},
        )(offsets, *rows, message, token, *below)[:4]

    def project(first, pieces, before, token, final=False):
        model = out_weight.shape[1]
        total = shape(rows_here // 4, model, dtype=BF16 if final else F32)
        scratch = [pltpu.VMEM((rows_here // 4, sum(x.shape[-1] for x in pieces)), BF16)]
        if final:
            scratch += [
                pltpu.VMEM((rows_here // 4, model), BF16),
                pltpu.SemaphoreType.DMA((model // 512,)),
            ]
        return call(
            functools.partial(project_kernel, first, len(before), final),
            [VMEM] * (len(pieces) + 1 + len(before)) + [ANY],
            total,
            "project%d" % first,
            scratch=scratch,
            out_spec=ANY if final else VMEM,
        )(*pieces, *before, weights, token)

    def both(members):
        cut = slice(members[0], members[-1] + 1)
        return jnp.stack([kv3[cut], kv3_near[cut]])

    def send(value, axis, pairs):
        return lax.ppermute(value, axis, pairs)

    group_a, group_b = GROUPS
    *rows_a, = own((0, 1), kv3)
    kv3_near, rows_a[1] = lax.optimization_barrier((kv3_near, rows_a[1]))
    far_a, kv2_a, q23 = lax.optimization_barrier((both(group_a), kv2[0], q23))
    rows_b = own((2, 3), far_a)
    far_a, kv2_a = send(far_a, "ctx", far), send(kv2_a, "ctx", near)
    q23 = send(q23, "ctx", swap)
    msg1, o1, s1 = lower((0, 1), first, rows_b[0])
    turn = send(msg1, "ctx", swap)
    *rows_b, weights = call(
        weights_kernel,
        [SMEM] + [VMEM] * 10 + [ANY],
        [state] * 4 + [shape(*out_weight.shape)],
        "weights",
        aliases={1 + i: i for i in range(4)},
    )(offsets, *rows_b, qt, kt, vt, o1, s1, out_weight, msg1)

    far_a, kv2_a, far_b, kv2_b, weights = lax.optimization_barrier(
        (far_a, kv2_a, both(group_b), kv2[1], weights)
    )
    ready = far_b
    far_b, kv2_b = send(far_b, "ctx", far), send(kv2_b, "ctx", near)
    column_a = [kv2_a, kv3_near, far_a]
    (msg_a,) = partner(group_a, column_a, ready, 1)
    got_a = send(msg_a, "ctx", swap)
    rows_a = list(mine(group_a, rows_a, column_a, msg_a))
    msg1c = call(
        last_kernel,
        [SMEM] + [VMEM] * 3 + [ANY],
        message(RES // 2),
        "last",
        scratch=[slab],
    )(offsets, turn, kt, vt, rows_a[0])
    got1c = send(msg1c, "ctx", swap)
    rows_a = finished(group_a, rows_a, got_a, msg1c, turn)
    a1, a23 = send(rows_a[1], "head", over[1]), send(rows_a[2], "head", over[2])

    column_b = [kv2_b, kv3_near, far_b]
    msg_b, msg_c = partner(group_b, column_b, rows_a[0], 2)
    got_b, got_c = send(msg_b, "ctx", swap), send(msg_c, "ctx", swap)
    rows_b = mine(group_b, rows_b, column_b, msg_c, "past")
    a23, *rows_b = lax.optimization_barrier((a23, *rows_b))
    a3 = send(a23[1], "head", over[1])
    rows_b, rows_c = rows_b[:2], rows_b[2:]
    rows_b = finished((2,), rows_b, got_b, rows_c[0], got1c)
    b1, b23 = send(rows_b[1], "head", over[1]), send(rows_b[2], "head", over[2])
    rows_c = finished((3,), rows_c, got_c, rows_b[0])
    c2, c3, c1 = (send(rows_c[t], "head", over[t]) for t in (2, 3, 1))
    half = project(0, [rows_a[0], a1, a23, a3, rows_b[0], b1], [], rows_c[0])
    b23, half = lax.optimization_barrier((b23, half))
    b3 = send(b23[1], "head", over[1])
    last = [b23, b3, rows_c[0], c1, c2, c3]
    return project(10 * DH, last, [half], half, final=True)


def solution(mesh):
    placed = (P("ctx", "head"), P("ctx", "head"), P("ctx", "head"), P(), P())
    return jax.shard_map(
        body, mesh=mesh, in_specs=placed, out_specs=P(("ctx", "head"), None), check_vma=False
    )
```
